32 devices in a mesh: row: 8 (over z, x), col: 4 (over y, core).
Axes of the slice: x: 2, y: 2, z: 4, core: 2. Of those that a mesh axis runs over, the one named last changes fastest.
Arguments:
- edge_vec: float32 [3, 256], P(None, ('row', 'col')), may hold values from -8 to 8
- edge_atoms: int32 [2, 256], P(None, ('row', 'col')), may hold values from 0 to 47
- block_weight: bfloat16 [144, 16384], replicated, may hold values from -0.5 to 0.5
- base_hamiltonian: bfloat16 [6144, 6144], P('row', 'col'), as said below
- lower_bound: float32 [1], replicated, may hold values from -50 to -40
- upper_bound: float32 [1], replicated, may hold values from 40 to 50
Outputs:
- purified: float32 [6144, 6144], P('row', 'col')
The draws below stay inside these ranges and needn't reach their ends.
Inputs may be any that keep to these rules, and one draw needn't show every extreme that they name: `base_hamiltonian`: symmetric.
All inputs are finite; a program needn't handle non-finite values.
Results may differ from the reference program's by a relative error of at most 0.0031.
Values may be sent and summed in bfloat16 or wider, within the bound.
No kernel may reach another device: no remote copies, remote signals or barrier semaphores. Data moves between devices by JAX's collectives and lax.ppermute only.
A program may use at most 192 MiB of HBM per device.

```python
import math
import jax
import jax.numpy as jnp
import numpy as np
from jax import lax

ORB = 128
NR = 16
FEAT = 144
NB = 48
NORB = 6144
EDGES = 256


def draw_base_hamiltonian(key, part):
    raw = jax.random.normal(key, (NORB, NORB), jnp.float32)
    return ((raw + raw.T) * 0.7071).astype(jnp.bfloat16)


def set_ends(array, stream_key, low, high):
    longest = array.shape.index(max(array.shape))
    spots = []
    for shift in (0, 1):
        where = [jax.random.randint(jax.random.fold_in(stream_key, axis), (), 0, length) for axis, length in enumerate(array.shape)]
        where[longest] = (where[longest] + shift) % array.shape[longest]
        spots.append(tuple(where))
    return array.at[spots[0]].set(low).at[spots[1]].set(high)


def levels(own_key, dims, shards, least, top_value):
    loudness = 1.0
    for axis_at, blocks in shards:
        draws = jax.random.uniform(jax.random.fold_in(jax.random.fold_in(own_key, 6), axis_at), (blocks,), jnp.float32, least / len(shards), top_value / len(shards))
        loudness = loudness * jnp.repeat(jnp.exp(draws), dims[axis_at] // blocks).reshape((-1,) + (1,) * (len(dims) - 1 - axis_at))
    return loudness


def cumulative_ranks(amount, slope):
    portions = [(1 << 20) // math.isqrt(rank ** slope) + 1 for rank in range(1, amount + 1)]
    deviation = 1 + sum(portions) // (1 << 30)
    return np.cumsum(np.array([max(1, weight // deviation) for weight in portions]))


def skewed_ids(key, extent, count, lean):
    table = cumulative_ranks(count, lean)
    ticket = jax.random.randint(jax.random.fold_in(key, 1), extent, 0, int(table[count - 1]))
    rank = jnp.searchsorted(jnp.asarray(table, jnp.int32), ticket, side="right")
    return jax.random.permutation(jax.random.fold_in(key, 2), count)[rank].astype(jnp.int32)


def noise(stream_key, extent, scale, reach, cuts=(), kind=jnp.bfloat16):
    gain = levels(stream_key, extent, cuts, -0.22, 0.18) if cuts else 1.0
    drawn = jax.random.normal(stream_key, extent, jnp.float32) * scale * gain
    return jnp.minimum(jnp.maximum(drawn, -reach), reach).astype(kind)


def setup_inputs(seed: int = 0) -> dict:
    arg_keys = jax.random.split(jax.random.key(seed), 7)
    return {
        "edge_vec": noise(arg_keys[0], (3, EDGES), 2.0, 8.0, ((1, 32),), jnp.float32),
        "edge_atoms": set_ends(skewed_ids(arg_keys[1], (2, EDGES), NB, 1), jax.random.fold_in(arg_keys[1], 3), 0, NB - 1).astype(jnp.int32),
        "block_weight": noise(arg_keys[2], (FEAT, ORB * ORB), FEAT ** -0.5, 0.5),
        "base_hamiltonian": draw_base_hamiltonian(jax.random.fold_in(arg_keys[6], 71), 0),
        "lower_bound": jnp.clip(jax.random.uniform(arg_keys[4], (1,), jnp.float32, -50.0, -40.0), -50.0, -40.0),
        "upper_bound": jnp.clip(jax.random.uniform(arg_keys[5], (1,), jnp.float32, 40.0, 50.0), 40.0, 50.0),
    }


def features(edge_vec):
    squared = lax.optimization_barrier(jnp.sum(edge_vec * edge_vec, axis=0))
    radius = jnp.sqrt(squared + 0.25)
    unit_x = edge_vec[0] / radius
    unit_y = edge_vec[1] / radius
    unit_z = edge_vec[2] / radius
    harmonics = jnp.stack([jnp.ones_like(unit_x), unit_x, unit_y, unit_z, unit_x * unit_y, unit_y * unit_z, unit_z * unit_x, unit_x * unit_x - unit_y * unit_y, 3.0 * unit_z * unit_z - 1.0])
    centers = 1.0 + 0.3 * jnp.arange(NR, dtype=jnp.float32)
    radial = jnp.exp(-jnp.square((radius[None, :] - centers[:, None]) / 0.5))
    return (radial[:, None, :] * harmonics[None, :, :]).reshape(NR * 9, edge_vec.shape[1])

def reference(edge_vec, edge_atoms, block_weight, base_hamiltonian, lower_bound, upper_bound):
    embedding = features(edge_vec)
    position = (edge_atoms[0] * NB + edge_atoms[1]).astype(jnp.int32)
    selector = (jnp.arange(NB * NB, dtype=jnp.int32)[:, None] == position[None, :]).astype(jnp.float32)
    coefficient = lax.dot_general(selector, embedding, (((1,), (1,)), ((), ())), precision=lax.Precision.HIGHEST)
    blocks = jnp.dot(coefficient.astype(jnp.bfloat16), block_weight, preferred_element_type=jnp.float32).reshape(NB, NB, ORB, ORB)
    hamiltonian = (blocks + blocks.transpose(1, 0, 3, 2)).transpose(0, 2, 1, 3).reshape(NORB, NORB)
    hamiltonian = hamiltonian + base_hamiltonian.astype(jnp.float32)
    index_rows = jnp.arange(NORB, dtype=jnp.int32)
    diagonal_mask = index_rows[:, None] == index_rows[None, :]
    shifted = jnp.where(diagonal_mask, upper_bound[0], jnp.float32(0.0)) - hamiltonian
    start_density = (shifted / (upper_bound[0] - lower_bound[0])).astype(jnp.bfloat16)
    density_wide = start_density.astype(jnp.float32)
    return jnp.dot(density_wide, density_wide, precision=lax.Precision.HIGHEST)
```

```python
import functools

import jax
import jax.numpy as jnp
from jax import lax
from jax.experimental import pallas as pl
from jax.experimental.pallas import tpu as pltpu
from jax.sharding import PartitionSpec as P

ORB = 128
NR = 16
AXES = ("row", "col")
VMEM_BYTES = 60 * 1024 * 1024
EDGE_CHUNK = 256


def features(edge_vec):
    squared = jnp.sum(edge_vec * edge_vec, axis=0)
    radius = jnp.sqrt(squared + 0.25)
    unit_x = edge_vec[0] / radius
    unit_y = edge_vec[1] / radius
    unit_z = edge_vec[2] / radius
    harmonics = jnp.stack(
        [
            jnp.ones_like(unit_x),
            unit_x,
            unit_y,
            unit_z,
            unit_x * unit_y,
            unit_y * unit_z,
            unit_z * unit_x,
            unit_x * unit_x - unit_y * unit_y,
            3.0 * unit_z * unit_z - 1.0,
        ]
    )
    centers = 1.0 + 0.3 * jnp.arange(NR, dtype=jnp.float32)
    radial = jnp.exp(-jnp.square((radius[None, :] - centers[:, None]) / 0.5))
    return (radial[:, None, :] * harmonics[None, :, :]).reshape(NR * 9, edge_vec.shape[1])


def gather_edges(packed, devices):
    current = packed
    bit = 1
    while bit < devices:
        arrived = lax.ppermute(current, AXES, [(d, d ^ bit) for d in range(devices)])
        current = jnp.concatenate([current, arrived], axis=1)
        bit *= 2
    return current


def correction_kernel(edges, chunks, atoms, corner, scale, coefficient, weight, out, blocks):
    strip = pl.program_id(0)
    chunk = pl.program_id(1)
    size = edges // chunks
    rows, cols = out.shape[1:]

    @pl.when((strip == 0) | (chunks > 1))
    def _():
        coef = coefficient[...]

        def expand(i, _):
            at = pl.multiple_of(i * ORB, ORB)
            blocks[pl.ds(i, size, stride=ORB), :] = jnp.dot(
                coef, weight[:, pl.ds(at, ORB)], preferred_element_type=jnp.float32
            )
            return 0

        lax.fori_loop(0, ORB, expand, 0)

    row_atom = corner[0, strip]
    col_atom = corner[1, strip]
    inverse = scale[1]

    @pl.when(chunk == 0)
    def _():
        def fill(i, _):
            at = pl.multiple_of(i * ORB, ORB)
            row_ids = row_atom * ORB + at + lax.broadcasted_iota(jnp.int32, (ORB, cols), 0)
            col_ids = col_atom * ORB + lax.broadcasted_iota(jnp.int32, (ORB, cols), 1)
            out[0, pl.ds(at, ORB), :] = jnp.where(row_ids == col_ids, scale[0], jnp.float32(0.0))
            return 0

        lax.fori_loop(0, rows // ORB, fill, 0)

    def scatter(e, _):
        first = atoms[0, chunk * size + e]
        second = atoms[1, chunk * size + e]
        at = pl.multiple_of(e * ORB, ORB)
        direct_row, direct_col = first - row_atom, second - col_atom
        mirror_row, mirror_col = second - row_atom, first - col_atom

        def inside(row, col):
            return (row >= 0) & (row < rows // ORB) & (col >= 0) & (col < cols // ORB) & (first >= 0)

        @pl.when(inside(direct_row, direct_col))
        def _():
            spot = (
                0,
                pl.ds(pl.multiple_of(direct_row * ORB, ORB), ORB),
                pl.ds(pl.multiple_of(direct_col * ORB, ORB), ORB),
            )
            out[spot] = out[spot] - blocks[pl.ds(at, ORB), :] * inverse

        @pl.when(inside(mirror_row, mirror_col))
        def _():
            spot = (
                0,
                pl.ds(pl.multiple_of(mirror_row * ORB, ORB), ORB),
                pl.ds(pl.multiple_of(mirror_col * ORB, ORB), ORB),
            )
            out[spot] = out[spot] - blocks[pl.ds(at, ORB), :].T * inverse

        return 0

    lax.fori_loop(0, size, scatter, 0)


def corrections(atoms, corner, scale, coefficient, weight, tile):
    edges, feat = coefficient.shape
    chunks = max(1, edges // EDGE_CHUNK)
    strips = corner.shape[1]
    return pl.pallas_call(
        functools.partial(correction_kernel, edges, chunks),
        out_shape=jax.ShapeDtypeStruct((strips,) + tile, jnp.float32),
        grid=(strips, chunks),
        in_specs=[
            pl.BlockSpec(memory_space=pltpu.SMEM),
            pl.BlockSpec(memory_space=pltpu.SMEM),
            pl.BlockSpec(memory_space=pltpu.SMEM),
            pl.BlockSpec((edges // chunks, feat), lambda s, c: (c, 0)),
            pl.BlockSpec(weight.shape, lambda s, c: (0, 0)),
        ],
        out_specs=pl.BlockSpec((1,) + tile, lambda s, c: (s, 0, 0)),
        scratch_shapes=[pltpu.VMEM((edges // chunks * ORB, ORB), jnp.float32)],
        compiler_params=pltpu.CompilerParams(vmem_limit_bytes=VMEM_BYTES),
    )(atoms, corner, scale, coefficient, weight)


def shards(row_size, col_size, edge_vec, edge_atoms, block_weight, base, lower_bound, upper_bound):
    devices = row_size * col_size
    half_rows = row_size // 2
    half_cols = col_size // 2
    tile_rows, tile_cols = base.shape
    cells = tile_cols // tile_rows
    row_atoms, col_atoms = tile_rows // ORB, tile_cols // ORB
    row = lax.axis_index("row")
    col = lax.axis_index("col")
    row_half, row_in = row // half_rows, row % half_rows
    col_half, col_in = col // half_cols, col % half_cols
    on_diagonal = row_half == col_half

    def moves(where):
        pairs = []
        for r in range(row_size):
            for c in range(col_size):
                to = where(r // half_rows, r % half_rows, c // half_cols, c % half_cols)
                if to is not None:
                    h, i, y, k = to
                    pairs.append((r * col_size + c, (h * half_rows + i) * col_size + y * half_cols + k))
        return pairs

    def send(value, where):
        return lax.ppermute(value, AXES, moves(where))

    packed = jnp.concatenate([edge_vec, edge_atoms.astype(jnp.float32)], axis=0)
    everyone = gather_edges(packed, devices)
    base, everyone = lax.optimization_barrier((base, everyone))

    strips = {0: base}
    for mask in range(1, half_rows):
        bits = [1 << b for b in range(half_rows.bit_length()) if mask >> b & 1]
        if len(bits) == 1:
            strips[mask] = send(base, lambda h, i, y, k: (h, i ^ mask, y, k))
            continue
        width = tile_cols // len(bits)
        parts = []
        for at, bit in enumerate(bits):
            piece = strips[mask ^ bit][:, at * width : (at + 1) * width]
            parts.append(send(piece, lambda h, i, y, k: (h, i ^ bit, y, k)))
        strips[mask] = jnp.concatenate(parts, axis=1)
    from_diagonal = send(base, lambda h, i, y, k: (h, i, 1 - y, k) if h == y else None)
    mine = jnp.where(on_diagonal, base, from_diagonal)
    tiles = {0: mine}
    for mask in range(1, half_cols):
        tiles[mask] = send(mine, lambda h, i, y, k: (h, i, y, k ^ mask))

    embedding = features(everyone[:3])
    pair_atoms = everyone[3:].astype(jnp.int32)
    atoms_total = row_atoms * row_size
    position = pair_atoms[0] * atoms_total + pair_atoms[1]
    same = position[:, None] == position[None, :]
    edges = position.shape[0]
    order = jnp.arange(edges, dtype=jnp.int32)
    earlier = jnp.any(same & (order[None, :] < order[:, None]), axis=1)
    coefficient = lax.dot_general(
        same.astype(jnp.float32), embedding, (((1,), (1,)), ((), ())), precision=lax.Precision.HIGHEST
    ).astype(jnp.bfloat16)
    pair_atoms = jnp.where(earlier[None, :], jnp.int32(-1), pair_atoms)
    span = upper_bound[0] - lower_bound[0]
    scale = jnp.stack([upper_bound[0] / span, 1.0 / span])
    corner_rows = jnp.concatenate(
        [
            (row_half * half_rows + jnp.arange(half_rows, dtype=jnp.int32)) * row_atoms,
            jnp.broadcast_to(row * row_atoms, (half_cols,)),
        ]
    )
    corner_cols = jnp.concatenate(
        [
            jnp.broadcast_to(col * col_atoms, (half_rows,)),
            (row_half * half_cols + jnp.arange(half_cols, dtype=jnp.int32)) * col_atoms,
        ]
    )
    corner = jnp.stack([corner_rows, corner_cols]).astype(jnp.int32)
    correction = corrections(pair_atoms, corner, scale, coefficient, block_weight, base.shape)

    def density(tile, corrected):
        return (corrected - tile.astype(jnp.float32) * scale[1]).astype(jnp.bfloat16)

    tall = jnp.zeros((half_rows, tile_rows, tile_cols), jnp.bfloat16)
    for mask in range(half_rows):
        at = row_in ^ mask
        value = density(strips[mask], lax.dynamic_index_in_dim(correction, at, 0, keepdims=False))
        tall = lax.dynamic_update_index_in_dim(tall, value, at, 0)
    tall = tall.reshape(half_rows * tile_rows, tile_cols)
    wide = jnp.zeros((tile_rows, half_cols * tile_cols), jnp.bfloat16)
    for mask in range(half_cols):
        at = col_in ^ mask
        value = density(tiles[mask], lax.dynamic_index_in_dim(correction, half_rows + at, 0, keepdims=False))
        wide = lax.dynamic_update_slice(wide, value, (0, at * tile_cols))

    near = jnp.dot(wide, tall, preferred_element_type=jnp.float32)
    total = near

    own = density(base, lax.dynamic_index_in_dim(correction, row_in, 0, keepdims=False))
    square = lax.dot_general(own, tall, (((1,), (1,)), ((), ())), preferred_element_type=jnp.float32)

    def columns_of(value, k):
        return lax.dynamic_slice(value, (0, k * tile_cols), (tile_rows, tile_cols))

    summed = columns_of(square, col_in)
    for mask in range(1, half_cols):
        part = columns_of(square, col_in ^ mask).astype(jnp.bfloat16)
        summed = summed + send(part, lambda h, i, y, k: (h, i, y, k ^ mask)).astype(jnp.float32)
    total = total + send(
        summed.astype(jnp.bfloat16), lambda h, i, y, k: (h, i, 1 - y, k) if h != y else None
    ).astype(jnp.float32)

    for turn in range(cells):
        slot = (row_in + turn) % cells
        cell = lax.dynamic_slice(near, (0, slot * tile_rows), (tile_rows, tile_rows)).astype(jnp.bfloat16)

        def opposite(h, i, y, k):
            return (1 - h, k * cells + (i + turn) % cells, h, i // cells)

        if turn % 2 == 0:
            arrived = send(cell, lambda h, i, y, k: opposite(h, i, y, k) if h != y else None)
        else:
            def relay(h, i, y, k):
                to = opposite(h, i, y, k)
                return (to[0], to[1], y, to[3])

            arrived = send(cell, lambda h, i, y, k: relay(h, i, y, k) if h != y else None)
            arrived = send(arrived, lambda h, i, y, k: (h, i, 1 - y, k) if h == y else None)
        spot = (row_in - turn) % cells
        spread = jnp.concatenate(
            [jnp.where(spot == s, arrived.T, jnp.zeros_like(arrived)) for s in range(cells)], axis=1
        )
        total = total + spread.astype(jnp.float32)
    return total


def solution(mesh):
    return jax.shard_map(
        functools.partial(shards, mesh.shape["row"], mesh.shape["col"]),
        mesh=mesh,
        in_specs=(P(None, AXES), P(None, AXES), P(), P("row", "col"), P(), P()),
        out_specs=P("row", "col"),
        check_vma=False,
    )
```

```python
import functools

import jax
import jax.numpy as jnp
from jax import lax
from jax.experimental import pallas as pl
from jax.experimental.pallas import tpu as pltpu
from jax.sharding import PartitionSpec as P

ORB = 128
NR = 16
AXES = ("row", "col")
VMEM_BYTES = 60 * 1024 * 1024
EDGE_CHUNK = 256
BYTES_PER_US = 1_500_000
STEPS = ((0,), 1, 0, (1,))
CUTS = (6, 0)
PLAN = {
    'density_b_across_rows_2': ('raw_a_across_rows_1', 'raw_a_across_rows_2', 'raw_a_beside'),
    'far_2_3_across_cores': ('near_1_beside',),
    'wide_across_cores': ('density_b_across_rows_1', 'density_b_across_rows_2'),
}


def taking(microseconds):
    return pl.CostEstimate(flops=0, bytes_accessed=int(microseconds * BYTES_PER_US), transcendentals=0)


def prepare_kernel(cells, chunks, atoms, atoms_total, edges, corner, coefficient, hits, embedding):
    count = edges.shape[1]
    size = count // chunks
    vec = edges[0:3, :]
    squared = vec[0:1] * vec[0:1] + vec[1:2] * vec[1:2] + vec[2:3] * vec[2:3]
    radius = jnp.sqrt(squared + 0.25)
    x, y, z = vec[0:1] / radius, vec[1:2] / radius, vec[2:3] / radius
    harmonics = jnp.concatenate(
        [jnp.ones_like(x), x, y, z, x * y, y * z, z * x, x * x - y * y, 3.0 * z * z - 1.0], axis=0
    )
    for k in range(NR):
        away = (radius - (1.0 + 0.3 * k)) / 0.5
        embedding[9 * k : 9 * k + 9, :] = jnp.exp(-(away * away)) * harmonics

    flipped = edges[...].T
    first, second = flipped[:, 3:4], flipped[:, 4:5]
    position = first * atoms_total + second
    position_row = edges[3:4, :] * atoms_total + edges[4:5, :]
    same = position == position_row
    coefficient[...] = lax.dot_general(
        same.astype(jnp.float32),
        embedding[...],
        (((1,), (1,)), ((), ())),
        precision=lax.Precision.HIGHEST,
        preferred_element_type=jnp.float32,
    ).astype(jnp.bfloat16)
    before = lax.broadcasted_iota(jnp.int32, (count, count), 1) < lax.broadcasted_iota(jnp.int32, (count, count), 0)
    repeated = jnp.max(jnp.where(same & before, 1.0, 0.0), axis=1, keepdims=True)

    mirrored = corner[2:3, :]
    row = first + mirrored * (second - first) - corner[0:1, :]
    col = second + mirrored * (first - second) - corner[1:2, :]
    limit = float(atoms)
    found = (row >= 0) & (row < limit) & (col >= 0) & (col < limit) & (corner[3:4, :] > 0) & (repeated < 0.5)
    found = jnp.where(found, 1.0, 0.0)
    lanes = lax.broadcasted_iota(jnp.int32, (1, ORB), 1).astype(jnp.float32)
    index = lax.broadcasted_iota(jnp.int32, (size, 1), 0).astype(jnp.float32)
    upto = lax.broadcasted_iota(jnp.int32, (size, size), 1) <= lax.broadcasted_iota(jnp.int32, (size, size), 0)
    upto = jnp.where(upto, 1.0, 0.0).astype(jnp.bfloat16)
    for chunk in range(chunks):
        part = slice(chunk * size, (chunk + 1) * size)
        here = found[part]
        place = jnp.dot(upto, here.astype(jnp.bfloat16), preferred_element_type=jnp.float32)
        code = (index * 2 + mirrored) * 4096 + row[part] * 64 + col[part]
        place = jnp.where(here > 0.5, place - 1.0, -1000.0)
        total = jnp.sum(here, axis=0, keepdims=True)
        for cell in range(cells):
            other = cells + cell
            direct = total[:, cell : cell + 1]
            at = jnp.where(place[:, cell : cell + 1] == lanes, code[:, cell : cell + 1], 0.0)
            at = at + jnp.where(place[:, other : other + 1] + direct == lanes, code[:, other : other + 1], 0.0)
            codes = jnp.sum(at, axis=0, keepdims=True)
            codes = jnp.where(lanes == ORB - 1, direct + total[:, other : other + 1], codes)
            hits[chunk, cell : cell + 1, :] = codes.astype(jnp.int32)


def prepare(edges, corner, atoms, atoms_total):
    count = edges.shape[1]
    chunks = max(1, count // EDGE_CHUNK)
    cells = corner.shape[1]
    once = jnp.concatenate([corner, jnp.zeros((1, cells), jnp.int32), jnp.ones((1, cells), jnp.int32)])
    twice = jnp.concatenate([corner, jnp.ones((2, cells), jnp.int32)])
    table = jnp.concatenate([once, twice], axis=1).astype(jnp.float32)
    table = jnp.pad(table, ((0, 4), (0, ORB - 2 * cells)))
    return pl.pallas_call(
        functools.partial(prepare_kernel, cells, chunks, atoms, atoms_total),
        out_shape=[
            jax.ShapeDtypeStruct((count, 9 * NR), jnp.bfloat16),
            jax.ShapeDtypeStruct((chunks, cells, ORB), jnp.int32),
        ],
        scratch_shapes=[pltpu.VMEM((9 * NR, count), jnp.float32)],
        cost_estimate=taking(3),
        compiler_params=pltpu.CompilerParams(vmem_limit_bytes=VMEM_BYTES),
    )(edges, table)


def density_kernel(chunks, cells, unread, base, hits, scale, corner, coefficient, weight, *refs):
    raw = refs[:cells]
    out = refs[cells + unread : 2 * cells + unread]
    raw_in, total, ready, blocks, sems = refs[2 * cells + unread :]
    size = coefficient.shape[0] // chunks
    side = total.shape[0]
    wide = 8
    pitch = ORB + 8
    copies = [pltpu.make_async_copy(raw[n], raw_in.at[n], sems.at[0, n]) for n in range(cells)]
    for copy in copies:
        copy.start()
    inverse = scale[1]

    def expand(chunk):
        def step(i, _):
            at = pl.multiple_of(i * (ORB * wide), ORB * wide)
            value = jnp.dot(
                coefficient[pl.ds(chunk * size, size), :],
                weight[:, pl.ds(at, ORB * wide)],
                preferred_element_type=jnp.float32,
            )
            for part in range(wide):
                blocks[pl.ds(i * wide + part, size, stride=pitch), :] = value[:, part * ORB : (part + 1) * ORB]
            return 0

        lax.fori_loop(0, ORB // wide, step, 0)

    if chunks == 1:
        expand(0)
    writes = []
    for n in range(cells):
        copies[n].wait()

        def spread(i, _):
            at = pl.ds(pl.multiple_of(i * ORB, ORB), ORB)
            total[at, :] = raw_in[n, at, :].astype(jnp.float32) * (-inverse)
            return 0

        lax.fori_loop(0, side // ORB, spread, 0)

        @pl.when(corner[0, base + n] == corner[1, base + n])
        def _():
            rows = lax.broadcasted_iota(jnp.int32, (ORB, ORB), 0)
            cols = lax.broadcasted_iota(jnp.int32, (ORB, ORB), 1)
            unit = jnp.where(rows == cols, scale[0], jnp.float32(0.0))
            for at in range(0, side, ORB):
                total[at : at + ORB, at : at + ORB] += unit

        for chunk in range(chunks):
            if chunks > 1:
                expand(chunk)

            def scatter(t, _):
                hit = hits[chunk, base + n, t]
                col = pl.multiple_of((hit % 64) * ORB, ORB)
                row = pl.multiple_of((hit // 64 % 64) * ORB, ORB)
                pair = hit // 4096
                spot = (pl.ds(row, ORB), pl.ds(col, ORB))
                block = blocks[pl.ds(pl.multiple_of(pair // 2 * pitch, 8), ORB), :] * inverse

                @pl.when(pair % 2 == 0)
                def _():
                    total[spot] = total[spot] - block

                @pl.when(pair % 2 == 1)
                def _():
                    total[spot] = total[spot] - block.T

                return 0

            lax.fori_loop(0, hits[chunk, base + n, ORB - 1], scatter, 0)

        def finish(i, _):
            at = pl.ds(pl.multiple_of(i * ORB, ORB), ORB)
            ready[n, at, :] = total[at, :].astype(jnp.bfloat16)
            return 0

        lax.fori_loop(0, side // ORB, finish, 0)
        writes.append(pltpu.make_async_copy(ready.at[n], out[n], sems.at[1, n]))
        writes[-1].start()
    for write in writes:
        write.wait()


def densities(raw, base, corner, hits, scale, coefficient, weight, sooner):
    cells = len(raw)
    side = raw[0].shape[0]
    edges = coefficient.shape[0]
    chunks = max(1, edges // EDGE_CHUNK)
    any_spec = pl.BlockSpec(memory_space=pl.ANY)
    return pl.pallas_call(
        functools.partial(density_kernel, chunks, cells, len(sooner), base),
        out_shape=[jax.ShapeDtypeStruct((side, side), jnp.bfloat16)] * cells,
        in_specs=[pl.BlockSpec(memory_space=pltpu.SMEM)] * 3
        + [pl.BlockSpec(memory_space=pltpu.VMEM)] * 2
        + [any_spec] * (cells + len(sooner)),
        out_specs=[any_spec] * cells,
        scratch_shapes=[
            pltpu.VMEM((cells, side, side), jnp.bfloat16),
            pltpu.VMEM((side, side), jnp.float32),
            pltpu.VMEM((cells, side, side), jnp.bfloat16),
            pltpu.VMEM((edges // chunks * (ORB + 8), ORB), jnp.float32),
            pltpu.SemaphoreType.DMA((2, cells)),
        ],
        cost_estimate=taking(6 + 2.5 * cells),
        compiler_params=pltpu.CompilerParams(vmem_limit_bytes=VMEM_BYTES),
    )(hits, scale, corner, coefficient, weight, *raw, *sooner)


def add_product(total, left, right, transposed, fresh):
    rows = total.shape[0]
    block = rows // 2
    contract = (((1,), (1,)), ((), ())) if transposed else (((1,), (0,)), ((), ()))
    for start in range(0, rows, block):
        at = pl.ds(start, block)
        value = lax.dot_general(left[at, :], right[...], contract, preferred_element_type=jnp.float32)
        total[at, :] = value if fresh else total[at, :] + value


def near_kernel(sides, sources, seeded, last, unread, source, *refs):
    count = len(sides)
    refs = list(refs)
    tall = [refs.pop(0) for _ in range(count)]
    wide = [refs.pop(0) for _ in range(sources)]
    seed = refs.pop(0) if seeded else None
    refs = refs[unread:]
    total = refs.pop(0)
    rounded = refs.pop(0) if last else None
    tall_in, wide_in, sems = refs
    waits = []
    for n in range(count):
        for s in range(sources):

            @pl.when(source[n] == s)
            def _():
                pltpu.make_async_copy(wide[s].at[sides[n]], wide_in.at[n], sems.at[n, 0]).start()

        here = [
            pltpu.make_async_copy(wide[0].at[sides[n]], wide_in.at[n], sems.at[n, 0]),
            pltpu.make_async_copy(tall[n], tall_in.at[n], sems.at[n, 1]),
        ]
        here[1].start()
        if seeded and n == 0:
            here.append(pltpu.make_async_copy(seed, total, sems.at[count, 0]))
            here[-1].start()
        waits.append(here)
    for n in range(count):
        for copy in waits[n]:
            copy.wait()
        add_product(total, wide_in.at[n], tall_in.at[n], False, n == 0 and not seeded)
    if last:
        rounded[...] = total[...].astype(jnp.bfloat16)


def near_share(source, tall, sides, wide, seed, last, sooner):
    cell = tall[0].shape
    sources = len(wide)
    count = len(tall)
    any_spec = pl.BlockSpec(memory_space=pl.ANY)
    operands = [source, *tall, *wide]
    if seed is not None:
        operands.append(seed)
    operands += sooner
    shapes = [jax.ShapeDtypeStruct(cell, jnp.float32)]
    if last:
        shapes.append(jax.ShapeDtypeStruct(cell, jnp.bfloat16))
    return pl.pallas_call(
        functools.partial(near_kernel, sides, sources, seed is not None, last, len(sooner)),
        out_shape=shapes,
        in_specs=[pl.BlockSpec(memory_space=pltpu.SMEM)] + [any_spec] * (len(operands) - 1),
        out_specs=[pl.BlockSpec(memory_space=pltpu.VMEM)] * len(shapes),
        scratch_shapes=[
            pltpu.VMEM((count,) + cell, jnp.bfloat16),
            pltpu.VMEM((count,) + cell, jnp.bfloat16),
            pltpu.SemaphoreType.DMA((count + 1, 2)),
        ],
        cost_estimate=taking(2 + 2.5 * count),
        compiler_params=pltpu.CompilerParams(vmem_limit_bytes=VMEM_BYTES),
    )(*operands)


def far_kernel(count, unread, *refs):
    cells = refs[: 2 + 2 * count]
    out, cells_in, total, sems = refs[2 + 2 * count + unread :]
    copies = [pltpu.make_async_copy(ref, cells_in.at[n], sems.at[n]) for n, ref in enumerate(cells)]
    for copy in copies:
        copy.start()
    copies[0].wait()
    copies[1].wait()
    for m in range(count):
        for q in range(2):
            n = 2 + 2 * m + q
            copies[n].wait()
            add_product(total, cells_in.at[q], cells_in.at[n], True, q == 0)
        out[m] = total[...].astype(jnp.bfloat16)


def far_share(own, tall, sooner):
    cell = own[0].shape
    count = len(tall) // 2
    items = 2 + 2 * count
    any_spec = pl.BlockSpec(memory_space=pl.ANY)
    return pl.pallas_call(
        functools.partial(far_kernel, count, len(sooner)),
        out_shape=jax.ShapeDtypeStruct((count,) + cell, jnp.bfloat16),
        in_specs=[any_spec] * (items + len(sooner)),
        out_specs=pl.BlockSpec(memory_space=pltpu.VMEM),
        scratch_shapes=[
            pltpu.VMEM((items,) + cell, jnp.bfloat16),
            pltpu.VMEM(cell, jnp.float32),
            pltpu.SemaphoreType.DMA((items,)),
        ],
        cost_estimate=taking(3 + 3 * count),
        compiler_params=pltpu.CompilerParams(vmem_limit_bytes=VMEM_BYTES),
    )(*own, *tall, *sooner)


def final_kernel(groups, pieces, slot, *refs):
    refs = list(refs)
    near = [refs.pop(0) for _ in range(2)]
    far = [refs.pop(0) for _ in range(groups)]
    opposite = [[refs.pop(0) for _ in range(n)] for n in pieces]
    out = refs.pop(0)
    turn = pl.program_id(0)
    block = 128
    for q in range(2):

        @pl.when(turn == q)
        def _():
            start = 0
            for piece in opposite[q]:
                rows = piece.shape[0]

                def step(n, _):
                    at = pl.ds(pl.multiple_of(n * block, block), block)
                    to = pl.ds(start, rows)
                    value = near[q][at, to]
                    for share in far:
                        value = value + share[q, at, to].astype(jnp.float32)
                    out[at, to] = value + piece[:, at].astype(jnp.float32).T
                    return 0

                lax.fori_loop(0, out.shape[0] // block, step, 0)
                start += rows


def final_sum(slot, near, far, opposite):
    side = near[0].shape[0]
    operands = [*near, *far, *opposite[0], *opposite[1]]
    return pl.pallas_call(
        functools.partial(final_kernel, len(far), [len(pieces) for pieces in opposite]),
        out_shape=jax.ShapeDtypeStruct((side, 2 * side), jnp.float32),
        grid_spec=pltpu.PrefetchScalarGridSpec(
            num_scalar_prefetch=1,
            grid=(2,),
            in_specs=[pl.BlockSpec(o.shape, lambda t, s, n=len(o.shape): (0,) * n) for o in operands],
            out_specs=pl.BlockSpec((side, side), lambda t, s: (0, s[t])),
        ),
        cost_estimate=taking(9),
        compiler_params=pltpu.CompilerParams(vmem_limit_bytes=VMEM_BYTES),
    )(slot, *operands)


def after(value, *earlier):
    return lax.optimization_barrier((value, *earlier))[0] if earlier else value


def shards(row_size, col_size, edge_vec, edge_atoms, block_weight, base, lower_bound, upper_bound):
    devices = row_size * col_size
    half_rows = row_size // 2
    half_cols = col_size // 2
    side = base.shape[0]
    atoms = side // ORB
    row = lax.axis_index("row")
    col = lax.axis_index("col")
    row_half, row_in = row // half_rows, row % half_rows
    col_half, col_in = col // half_cols, col % half_cols
    on_diagonal = row_half == col_half
    slots = jnp.stack([row_in % 2, 1 - row_in % 2]).astype(jnp.int32)

    def moves(where):
        pairs = []
        for r in range(row_size):
            for c in range(col_size):
                to = where(r // half_rows, r % half_rows, c // half_cols, c % half_cols)
                if to is not None:
                    h, i, y, k = to
                    pairs.append((r * col_size + c, (h * half_rows + i) * col_size + y * half_cols + k))
        return pairs

    made = {}

    def waits(what):
        return [made[name] for name in PLAN.get(what, ()) if name in made]

    def send(value, where, what):
        with jax.named_scope(what):
            made[what] = lax.ppermute(after(value, *waits(what)), AXES, moves(where))
        return made[what]

    def swap_rows(value, bit, what):
        return send(value, lambda h, i, y, k: (h, i ^ bit, y, k), f"{what}_across_rows_{bit}")

    def to_beside(value, from_diagonal, what):
        return send(value, lambda h, i, y, k: (h, i, 1 - y, k) if (h == y) == from_diagonal else None, what)

    raw = [lax.dynamic_slice(base, (0, slots[q] * side), (side, side)) for q in range(2)]
    singles = [1 << b for b in range(half_rows.bit_length() - 1)]
    others = [m for m in range(1, half_rows) if m & (m - 1)]

    edges = jnp.concatenate(
        [edge_vec, edge_atoms.astype(jnp.float32), jnp.zeros((3, edge_vec.shape[1]), jnp.float32)], axis=0
    )
    raw_a = {0: raw[0]}

    def double(value, bit):
        arrived = lax.ppermute(value, AXES, [(d, d ^ bit) for d in range(devices)])
        return jnp.concatenate([value, arrived], axis=1)

    bit = devices // 2
    while bit > col_size:
        edges = double(edges, bit)
        bit //= 2
    for mask in singles[1:]:
        raw_a[mask] = swap_rows(after(raw[0], edges), mask, "raw_a")
    edges = double(edges, col_size)
    raw_a[1] = swap_rows(after(raw[1], edges), 1, "raw_a")
    bit = col_size // 2
    while bit >= half_cols:
        edges = double(edges, bit)
        bit //= 2
    beside_a = to_beside(after(raw[0], edges), True, "raw_a_beside")
    while bit:
        edges = double(edges, bit)
        bit //= 2

    span = upper_bound[0] - lower_bound[0]
    scale = jnp.stack([upper_bound[0] / span, 1.0 / span])

    done = []
    sums = []
    beside = []

    def tall_corner(mask, q):
        return row_half * half_rows + (row_in ^ mask), 2 * col + slots[q]

    corners = [tall_corner(0, q) for q in range(2)] + [tall_corner(m, 0) for m in singles]
    corners += [(row, row_half * half_rows + 2 * col_in + slots[0])]
    corner = jnp.stack([jnp.stack([c[n] for c in corners]) for n in range(2)]).astype(jnp.int32) * atoms
    coefficient, hits = prepare(edges, corner, atoms, atoms * row_size)

    def density(cells, at):
        what = f"density_{at}"
        with jax.named_scope(what):
            got = densities(cells, at, corner, hits, scale, coefficient, block_weight, [*done[-1:], *waits(what)])
        done.append(got[0])
        return got

    tall = {mask: [None, None] for mask in range(half_rows)}
    def near_part(q):
        what = f"near_{q}"
        source = jnp.stack([(row_in // 2) ^ col_in ^ (m // 2) for m in range(half_rows)]).astype(jnp.int32)
        sides = tuple(m % 2 for m in range(half_rows))
        with jax.named_scope(what):
            got = near_share(source, [tall[m][q] for m in tall], sides, wide, None, True, [*done[-1:], *waits(what)])
        done.append(got[0])
        made[what] = got[1]
        return got

    def far_product(masks):
        what = "far_" + "_".join(map(str, masks))
        with jax.named_scope(what):
            part = far_share(own, [tall[m][q] for m in masks for q in range(2)], [*done[-1:], *waits(what)])
        done.append(part)
        made[what] = part
        return part

    def far_sum(masks, part):
        what = "far_" + "_".join(map(str, masks))
        owner = lambda i: (i // 2) ^ (masks[0] // 2)
        summed = part.astype(jnp.float32)
        for turn in range(1, half_cols):
            arrived = send(
                part,
                lambda h, i, y, k: (h, i, y, owner(i)) if h != y and k == owner(i) ^ turn else None,
                what + "_across_cores",
            )
            summed = summed + arrived.astype(jnp.float32)
        return send(
            summed.astype(jnp.bfloat16),
            lambda h, i, y, k: (h, i, 1 - y, k) if h != y and k == owner(i) else None,
            what + "_beside",
        )

    tall[0] = density(raw, 0)
    own = tall[0]
    tall[1][1] = swap_rows(own[0], 1, "density_b")
    beside_b = to_beside(own[1], True, "density_b_beside")
    mine_a = jnp.where(on_diagonal, raw[0], beside_a)
    for mask in singles[1:]:
        tall[mask][1] = swap_rows(own[1], mask, "density_b")
    got = density([raw_a[m] for m in singles] + [mine_a], 2)
    for mask, value in zip(singles, got):
        tall[mask][0] = value
    wide = [jnp.stack([got[len(singles)], jnp.where(on_diagonal, own[1], beside_b)])]
    for turn in range(1, half_cols):
        wide.append(send(wide[0], lambda h, i, y, k: (h, i, y, k ^ turn), "wide_across_cores"))
    for mask in others:
        bit = 1 if mask ^ 1 in singles else mask & ~1 & -(mask & ~1)
        tall[mask][1] = swap_rows(tall[mask ^ bit][0 if bit == 1 else 1], bit, "forward_b")
        bit = 1 << (mask.bit_length() - 1)
        tall[mask][0] = swap_rows(tall[mask ^ bit][0], bit, "forward_a")

    def opposite(h, i, y, k, turn):
        return (1 - h, k * 2 + (i + turn) % 2, h, i // 2)

    def exchange(value, turn, cut):
        across = lambda h, i, y, k: opposite(h, i, y, k, turn) if h != y else None
        onward = lambda h, i, y, k: opposite(h, i, 1 - y, k, turn) if h == y else None
        pieces = []
        if cut > 0:
            pieces.append(send(value[:cut], across, f"near_{turn}_direct"))
        if cut < side:
            ahead = to_beside(value[cut:], False, f"near_{turn}_beside")
            pieces.append(send(ahead, onward, f"near_{turn}_ahead"))
        return pieces

    near, got, parts, far = {}, {}, [], []
    for step in STEPS:
        if isinstance(step, int):
            near[step], value = near_part(step)
            got[step] = exchange(value, step, CUTS[step] * side // 6)
        else:
            for m in range(0, half_rows, 2):
                if min(m // 2, 1) in step:
                    parts.append(([m, m + 1], far_product([m, m + 1])))
    for masks, part in parts:
        far.append(far_sum(masks, part))
    return final_sum(slots, [near[0], near[1]], far, [got[0], got[1]])


def solution(mesh):
    return jax.shard_map(
        functools.partial(shards, mesh.shape["row"], mesh.shape["col"]),
        mesh=mesh,
        in_specs=(P(None, AXES), P(None, AXES), P(), P("row", "col"), P(), P()),
        out_specs=P("row", "col"),
        check_vma=False,
    )
```

```python
import functools

import jax
import jax.numpy as jnp
from jax import lax
from jax.experimental import pallas as pl
from jax.experimental.pallas import tpu as pltpu
from jax.sharding import PartitionSpec as P

ORB = 128
NR = 16
AXES = ("row", "col")
VMEM_BYTES = 127 * 512 * 1024
EDGE_CHUNK = 256
BYTES_PER_US = 1_500_000
STEPS = ((0,), 1, 0, (1,))
CUTS = (6, 0)
PLAN = {
    'density_b_across_rows_2': ('raw_a_across_rows_1', 'raw_a_across_rows_2', 'raw_a_beside'),
    'far_2_3_across_cores': ('near_1_beside',),
    'wide_b_across_cores': ('density_b_across_rows_1', 'density_b_across_rows_2'),
}


def taking(microseconds):
    return pl.CostEstimate(flops=0, bytes_accessed=int(microseconds * BYTES_PER_US), transcendentals=0)


def prepare_kernel(cells, chunks, atoms, atoms_total, edges, corner, coefficient, hits, embedding):
    count = edges.shape[1]
    size = count // chunks
    vec = edges[0:3, :]
    squared = vec[0:1] * vec[0:1] + vec[1:2] * vec[1:2] + vec[2:3] * vec[2:3]
    radius = jnp.sqrt(squared + 0.25)
    x, y, z = vec[0:1] / radius, vec[1:2] / radius, vec[2:3] / radius
    harmonics = jnp.concatenate(
        [jnp.ones_like(x), x, y, z, x * y, y * z, z * x, x * x - y * y, 3.0 * z * z - 1.0], axis=0
    )
    for k in range(NR):
        away = (radius - (1.0 + 0.3 * k)) / 0.5
        embedding[9 * k : 9 * k + 9, :] = jnp.exp(-(away * away)) * harmonics

    flipped = edges[...].T
    first, second = flipped[:, 3:4], flipped[:, 4:5]
    position = first * atoms_total + second
    position_row = edges[3:4, :] * atoms_total + edges[4:5, :]
    same = position == position_row
    coefficient[...] = lax.dot_general(
        same.astype(jnp.float32),
        embedding[...],
        (((1,), (1,)), ((), ())),
        precision=lax.Precision.HIGHEST,
        preferred_element_type=jnp.float32,
    ).astype(jnp.bfloat16)
    before = lax.broadcasted_iota(jnp.int32, (count, count), 1) < lax.broadcasted_iota(jnp.int32, (count, count), 0)
    repeated = jnp.max(jnp.where(same & before, 1.0, 0.0), axis=1, keepdims=True)

    mirrored = corner[2:3, :]
    row = first + mirrored * (second - first) - corner[0:1, :]
    col = second + mirrored * (first - second) - corner[1:2, :]
    limit = float(atoms)
    found = (row >= 0) & (row < limit) & (col >= 0) & (col < limit) & (corner[3:4, :] > 0) & (repeated < 0.5)
    found = jnp.where(found, 1.0, 0.0)
    lanes = lax.broadcasted_iota(jnp.int32, (1, ORB), 1).astype(jnp.float32)
    index = lax.broadcasted_iota(jnp.int32, (size, 1), 0).astype(jnp.float32)
    upto = lax.broadcasted_iota(jnp.int32, (size, size), 1) <= lax.broadcasted_iota(jnp.int32, (size, size), 0)
    upto = jnp.where(upto, 1.0, 0.0).astype(jnp.bfloat16)
    for chunk in range(chunks):
        part = slice(chunk * size, (chunk + 1) * size)
        here = found[part]
        place = jnp.dot(upto, here.astype(jnp.bfloat16), preferred_element_type=jnp.float32)
        code = (index * 2 + mirrored) * 4096 + row[part] * 64 + col[part]
        place = jnp.where(here > 0.5, place - 1.0, -1000.0)
        total = jnp.sum(here, axis=0, keepdims=True)
        for cell in range(cells):
            other = cells + cell
            direct = total[:, cell : cell + 1]
            at = jnp.where(place[:, cell : cell + 1] == lanes, code[:, cell : cell + 1], 0.0)
            at = at + jnp.where(place[:, other : other + 1] + direct == lanes, code[:, other : other + 1], 0.0)
            codes = jnp.sum(at, axis=0, keepdims=True)
            codes = jnp.where(lanes == ORB - 1, direct + total[:, other : other + 1], codes)
            hits[chunk, cell : cell + 1, :] = codes.astype(jnp.int32)


def cell_table(corner):
    cells = corner.shape[1]
    once = jnp.concatenate([corner, jnp.zeros((1, cells), jnp.int32), jnp.ones((1, cells), jnp.int32)])
    twice = jnp.concatenate([corner, jnp.ones((2, cells), jnp.int32)])
    table = jnp.concatenate([once, twice], axis=1).astype(jnp.float32)
    return jnp.pad(table, ((0, 4), (0, ORB - 2 * cells)))


def prepare(edges, table, cells, atoms, atoms_total):
    count = edges.shape[1]
    chunks = max(1, count // EDGE_CHUNK)
    return pl.pallas_call(
        functools.partial(prepare_kernel, cells, chunks, atoms, atoms_total),
        out_shape=[
            jax.ShapeDtypeStruct((count, 9 * NR), jnp.bfloat16),
            jax.ShapeDtypeStruct((chunks, cells, ORB), jnp.int32),
        ],
        scratch_shapes=[pltpu.VMEM((9 * NR, count), jnp.float32)],
        cost_estimate=taking(3),
        compiler_params=pltpu.CompilerParams(vmem_limit_bytes=VMEM_BYTES),
    )(edges, table)


def density_kernel(chunks, cells, unread, base, hits, scale, corner, coefficient, weight, *refs):
    raw = refs[:cells]
    out = refs[cells + unread : 2 * cells + unread]
    raw_in, total, ready, blocks, sems = refs[2 * cells + unread :]
    size = coefficient.shape[0] // chunks
    side = total.shape[0]
    wide = 8
    pitch = ORB + 8
    copies = [pltpu.make_async_copy(raw[n], raw_in.at[n], sems.at[0, n]) for n in range(cells)]
    for copy in copies:
        copy.start()
    inverse = scale[1]

    def expand(chunk):
        def step(i, _):
            at = pl.multiple_of(i * (ORB * wide), ORB * wide)
            value = jnp.dot(
                coefficient[pl.ds(chunk * size, size), :],
                weight[:, pl.ds(at, ORB * wide)],
                preferred_element_type=jnp.float32,
            )
            for part in range(wide):
                blocks[pl.ds(i * wide + part, size, stride=pitch), :] = value[:, part * ORB : (part + 1) * ORB]
            return 0

        lax.fori_loop(0, ORB // wide, step, 0)

    if chunks == 1:
        expand(0)
    writes = []
    for n in range(cells):
        copies[n].wait()

        def spread(i, _):
            at = pl.ds(pl.multiple_of(i * ORB, ORB), ORB)
            total[at, :] = raw_in[n, at, :].astype(jnp.float32) * (-inverse)
            return 0

        lax.fori_loop(0, side // ORB, spread, 0)

        @pl.when(corner[0, base + n] == corner[1, base + n])
        def _():
            rows = lax.broadcasted_iota(jnp.int32, (ORB, ORB), 0)
            cols = lax.broadcasted_iota(jnp.int32, (ORB, ORB), 1)
            unit = jnp.where(rows == cols, scale[0], jnp.float32(0.0))
            for at in range(0, side, ORB):
                total[at : at + ORB, at : at + ORB] += unit

        for chunk in range(chunks):
            if chunks > 1:
                expand(chunk)

            def scatter(t, _):
                hit = hits[chunk, base + n, t]
                col = pl.multiple_of((hit % 64) * ORB, ORB)
                row = pl.multiple_of((hit // 64 % 64) * ORB, ORB)
                pair = hit // 4096
                spot = (pl.ds(row, ORB), pl.ds(col, ORB))
                block = blocks[pl.ds(pl.multiple_of(pair // 2 * pitch, 8), ORB), :] * inverse

                @pl.when(pair % 2 == 0)
                def _():
                    total[spot] = total[spot] - block

                @pl.when(pair % 2 == 1)
                def _():
                    total[spot] = total[spot] - block.T

                return 0

            lax.fori_loop(0, hits[chunk, base + n, ORB - 1], scatter, 0)

        def finish(i, _):
            at = pl.ds(pl.multiple_of(i * ORB, ORB), ORB)
            ready[n, at, :] = total[at, :].astype(jnp.bfloat16)
            return 0

        lax.fori_loop(0, side // ORB, finish, 0)
        writes.append(pltpu.make_async_copy(ready.at[n], out[n], sems.at[1, n]))
        writes[-1].start()
    for write in writes:
        write.wait()


def densities(raw, base, corner, hits, scale, coefficient, weight, sooner):
    cells = len(raw)
    side = raw[0].shape[0]
    edges = coefficient.shape[0]
    chunks = max(1, edges // EDGE_CHUNK)
    any_spec = pl.BlockSpec(memory_space=pl.ANY)
    return pl.pallas_call(
        functools.partial(density_kernel, chunks, cells, len(sooner), base),
        out_shape=[jax.ShapeDtypeStruct((side, side), jnp.bfloat16)] * cells,
        in_specs=[pl.BlockSpec(memory_space=pltpu.SMEM)] * 3
        + [pl.BlockSpec(memory_space=pltpu.VMEM)] * 2
        + [any_spec] * (cells + len(sooner)),
        out_specs=[any_spec] * cells,
        scratch_shapes=[
            pltpu.VMEM((cells, side, side), jnp.bfloat16),
            pltpu.VMEM((side, side), jnp.float32),
            pltpu.VMEM((cells, side, side), jnp.bfloat16),
            pltpu.VMEM((edges // chunks * (ORB + 8), ORB), jnp.float32),
            pltpu.SemaphoreType.DMA((2, cells)),
        ],
        cost_estimate=taking(6 + 2.5 * cells),
        compiler_params=pltpu.CompilerParams(vmem_limit_bytes=VMEM_BYTES),
    )(hits, scale, corner, coefficient, weight, *raw, *sooner)


def add_product(total, left, right, transposed, fresh):
    rows = total.shape[0]
    block = rows // 2
    contract = (((1,), (1,)), ((), ())) if transposed else (((1,), (0,)), ((), ()))
    for start in range(0, rows, block):
        at = pl.ds(start, block)
        value = lax.dot_general(left[at, :], right[...], contract, preferred_element_type=jnp.float32)
        total[at, :] = value if fresh else total[at, :] + value


def near_kernel(sides, sources, seeded, last, unread, source, *refs):
    count = len(sides)
    refs = list(refs)
    tall = [refs.pop(0) for _ in range(count)]
    wide = [[refs.pop(0) for _ in range(sources)] for _ in range(2)]
    seed = refs.pop(0) if seeded else None
    refs = refs[unread:]
    total = refs.pop(0)
    rounded = refs.pop(0) if last else None
    tall_in, wide_in, sems = refs
    waits = []
    for n in range(count):
        for s in range(sources):

            @pl.when(source[n] == s)
            def _():
                pltpu.make_async_copy(wide[sides[n]][s], wide_in.at[n], sems.at[n, 0]).start()

        here = [
            pltpu.make_async_copy(wide[sides[n]][0], wide_in.at[n], sems.at[n, 0]),
            pltpu.make_async_copy(tall[n], tall_in.at[n], sems.at[n, 1]),
        ]
        here[1].start()
        if seeded and n == 0:
            here.append(pltpu.make_async_copy(seed, total, sems.at[count, 0]))
            here[-1].start()
        waits.append(here)
    for n in range(count):
        for copy in waits[n]:
            copy.wait()
        add_product(total, wide_in.at[n], tall_in.at[n], False, n == 0 and not seeded)
    if last:
        rounded[...] = total[...].astype(jnp.bfloat16)


def near_share(source, tall, sides, wide, seed, last, sooner):
    cell = tall[0].shape
    sources = len(wide[0])
    count = len(tall)
    any_spec = pl.BlockSpec(memory_space=pl.ANY)
    operands = [source, *tall, *wide[0], *wide[1]]
    if seed is not None:
        operands.append(seed)
    operands += sooner
    shapes = [jax.ShapeDtypeStruct(cell, jnp.float32)]
    if last:
        shapes.append(jax.ShapeDtypeStruct(cell, jnp.bfloat16))
    return pl.pallas_call(
        functools.partial(near_kernel, sides, sources, seed is not None, last, len(sooner)),
        out_shape=shapes,
        in_specs=[pl.BlockSpec(memory_space=pltpu.SMEM)] + [any_spec] * (len(operands) - 1),
        out_specs=[pl.BlockSpec(memory_space=pltpu.VMEM)] * len(shapes),
        scratch_shapes=[
            pltpu.VMEM((count,) + cell, jnp.bfloat16),
            pltpu.VMEM((count,) + cell, jnp.bfloat16),
            pltpu.SemaphoreType.DMA((count + 1, 2)),
        ],
        cost_estimate=taking(2 + 2.5 * count),
        compiler_params=pltpu.CompilerParams(vmem_limit_bytes=VMEM_BYTES),
    )(*operands)


def far_kernel(count, unread, *refs):
    cells = refs[: 2 + 2 * count]
    out, cells_in, total, sems = refs[2 + 2 * count + unread :]
    copies = [pltpu.make_async_copy(ref, cells_in.at[n], sems.at[n]) for n, ref in enumerate(cells)]
    for copy in copies:
        copy.start()
    copies[0].wait()
    copies[1].wait()
    for m in range(count):
        for q in range(2):
            n = 2 + 2 * m + q
            copies[n].wait()
            add_product(total, cells_in.at[q], cells_in.at[n], True, q == 0)
        out[m] = total[...].astype(jnp.bfloat16)


def far_share(own, tall, sooner):
    cell = own[0].shape
    count = len(tall) // 2
    items = 2 + 2 * count
    any_spec = pl.BlockSpec(memory_space=pl.ANY)
    return pl.pallas_call(
        functools.partial(far_kernel, count, len(sooner)),
        out_shape=jax.ShapeDtypeStruct((count,) + cell, jnp.bfloat16),
        in_specs=[any_spec] * (items + len(sooner)),
        out_specs=pl.BlockSpec(memory_space=pltpu.VMEM),
        scratch_shapes=[
            pltpu.VMEM((items,) + cell, jnp.bfloat16),
            pltpu.VMEM(cell, jnp.float32),
            pltpu.SemaphoreType.DMA((items,)),
        ],
        cost_estimate=taking(3 + 3 * count),
        compiler_params=pltpu.CompilerParams(vmem_limit_bytes=VMEM_BYTES),
    )(*own, *tall, *sooner)


def final_kernel(parts, pieces, slot, *refs):
    refs = list(refs)
    near = [refs.pop(0) for _ in range(2)]
    far = [[refs.pop(0) for _ in range(n)] for n in parts]
    opposite = [[refs.pop(0) for _ in range(n)] for n in pieces]
    out = refs.pop(0)
    turn = pl.program_id(0)
    block = 128
    for q in range(2):

        @pl.when(turn == q)
        def _():
            start = 0
            for piece in opposite[q]:
                rows = piece.shape[0]

                def step(n, _):
                    at = pl.ds(pl.multiple_of(n * block, block), block)
                    to = pl.ds(start, rows)
                    value = near[q][at, to]
                    for share in far:
                        part = share[q][0, at, to] if len(share) == 2 else share[0][q, at, to]
                        value = value + part.astype(jnp.float32)
                    out[at, to] = value + piece[:, at].astype(jnp.float32).T
                    return 0

                lax.fori_loop(0, out.shape[0] // block, step, 0)
                start += rows


def final_sum(slot, near, far, opposite):
    side = near[0].shape[0]
    operands = [*near, *[part for share in far for part in share], *opposite[0], *opposite[1]]
    return pl.pallas_call(
        functools.partial(final_kernel, [len(share) for share in far], [len(pieces) for pieces in opposite]),
        out_shape=jax.ShapeDtypeStruct((side, 2 * side), jnp.float32),
        grid_spec=pltpu.PrefetchScalarGridSpec(
            num_scalar_prefetch=1,
            grid=(2,),
            in_specs=[pl.BlockSpec(o.shape, lambda t, s, n=len(o.shape): (0,) * n) for o in operands],
            out_specs=pl.BlockSpec((side, side), lambda t, s: (0, s[t])),
        ),
        cost_estimate=taking(9),
        compiler_params=pltpu.CompilerParams(vmem_limit_bytes=VMEM_BYTES),
    )(slot, *operands)


def after(value, *earlier):
    return lax.optimization_barrier((value, *earlier))[0] if earlier else value


def shards(row_size, col_size, edge_vec, edge_atoms, block_weight, base, lower_bound, upper_bound):
    devices = row_size * col_size
    half_rows = row_size // 2
    half_cols = col_size // 2
    side = base.shape[0]
    atoms = side // ORB
    row = lax.axis_index("row")
    col = lax.axis_index("col")
    row_half, row_in = row // half_rows, row % half_rows
    col_half, col_in = col // half_cols, col % half_cols
    on_diagonal = row_half == col_half
    slots = jnp.stack([row_in % 2, 1 - row_in % 2]).astype(jnp.int32)

    def moves(where):
        pairs = []
        for r in range(row_size):
            for c in range(col_size):
                to = where(r // half_rows, r % half_rows, c // half_cols, c % half_cols)
                if to is not None:
                    h, i, y, k = to
                    pairs.append((r * col_size + c, (h * half_rows + i) * col_size + y * half_cols + k))
        return pairs

    made = {}

    def waits(what):
        return [made[name] for name in PLAN.get(what, ()) if name in made]

    def send(value, where, what):
        with jax.named_scope(what):
            made[what] = lax.ppermute(after(value, *waits(what)), AXES, moves(where))
        return made[what]

    def swap_rows(value, bit, what):
        return send(value, lambda h, i, y, k: (h, i ^ bit, y, k), f"{what}_across_rows_{bit}")

    def to_beside(value, from_diagonal, what):
        return send(value, lambda h, i, y, k: (h, i, 1 - y, k) if (h == y) == from_diagonal else None, what)

    raw = [lax.dynamic_slice(base, (0, slots[q] * side), (side, side)) for q in range(2)]
    singles = [1 << b for b in range(half_rows.bit_length() - 1)]
    others = [m for m in range(1, half_rows) if m & (m - 1)]

    span = upper_bound[0] - lower_bound[0]
    scale = jnp.stack([upper_bound[0] / span, 1.0 / span])

    def tall_corner(mask, q):
        return row_half * half_rows + (row_in ^ mask), 2 * col + slots[q]

    corners = [tall_corner(0, q) for q in range(2)] + [tall_corner(m, 0) for m in singles]
    corners += [(row, row_half * half_rows + 2 * col_in + slots[0])]
    corner = jnp.stack([jnp.stack([c[n] for c in corners]) for n in range(2)]).astype(jnp.int32) * atoms
    table = cell_table(corner)

    edges = jnp.concatenate(
        [edge_vec, edge_atoms.astype(jnp.float32), jnp.zeros((3, edge_vec.shape[1]), jnp.float32)], axis=0
    )
    raw_a = {0: raw[0]}

    def double(value, bit):
        arrived = lax.ppermute(value, AXES, [(d, d ^ bit) for d in range(devices)])
        return jnp.concatenate([value, arrived], axis=1)

    bit = devices // 2
    while bit > col_size:
        edges = double(edges, bit)
        bit //= 2
        edges = after(edges, *((raw[0], raw[1]) if bit == col_size else (table, scale, corner)))
    for mask in singles[1:]:
        raw_a[mask] = swap_rows(after(raw[0], edges), mask, "raw_a")
    edges = double(edges, col_size)
    raw_a[1] = swap_rows(after(raw[1], edges), 1, "raw_a")
    bit = col_size // 2
    while bit >= half_cols:
        edges = double(edges, bit)
        bit //= 2
    beside_a = to_beside(after(raw[0], edges), True, "raw_a_beside")
    while bit:
        edges = double(edges, bit)
        bit //= 2

    done = []
    sums = []
    beside = []

    coefficient, hits = prepare(edges, table, len(corners), atoms, atoms * row_size)

    def density(cells, at):
        what = f"density_{at}"
        with jax.named_scope(what):
            got = densities(cells, at, corner, hits, scale, coefficient, block_weight, [*done[-1:], *waits(what)])
        done.append(got[0])
        return got

    tall = {mask: [None, None] for mask in range(half_rows)}
    def near_part(q):
        what = f"near_{q}"
        place = after((row_in // 2) ^ col_in, *waits(what + "_source"))
        source = jnp.stack([place ^ (m // 2) for m in range(half_rows)]).astype(jnp.int32)
        sides = tuple(m % 2 for m in range(half_rows))
        with jax.named_scope(what):
            got = near_share(source, [tall[m][q] for m in tall], sides, wide, None, True, [*done[-1:], *waits(what)])
        done.append(got[0])
        made[what] = got[1]
        return got

    def far_product(masks):
        what = "far_" + "_".join(map(str, masks))
        with jax.named_scope(what):
            part = far_share(own, [tall[m][q] for m in masks for q in range(2)], [*done[-1:], *waits(what)])
        done.append(part)
        made[what] = part
        return part

    def far_sum(masks, part):
        what = "far_" + "_".join(map(str, masks))
        owner = lambda i: (i // 2) ^ (masks[0] // 2)
        summed = part.astype(jnp.float32)
        for turn in range(1, half_cols):
            arrived = send(
                part,
                lambda h, i, y, k: (h, i, y, owner(i)) if h != y and k == owner(i) ^ turn else None,
                what + "_across_cores",
            )
            summed = summed + arrived.astype(jnp.float32)
        across = lambda h, i, y, k: (h, i, 1 - y, k) if h != y and k == owner(i) else None
        summed = summed.astype(jnp.bfloat16)
        if masks[0] == 0:
            return [send(summed, across, f"{what}_beside")]
        return [send(summed[n : n + 1], across, f"{what}_beside_{n}") for n in range(2)]

    tall[0] = density(raw, 0)
    own = tall[0]
    tall[1][1] = swap_rows(own[0], 1, "density_b")
    beside_b = to_beside(own[1], True, "density_b_beside")
    mine_a = jnp.where(on_diagonal, raw[0], beside_a)
    for mask in singles[1:]:
        tall[mask][1] = swap_rows(own[1], mask, "density_b")
    got = density([raw_a[m] for m in singles] + [mine_a], 2)
    for mask, value in zip(singles, got):
        tall[mask][0] = value
    wide = [[got[len(singles)]], [jnp.where(on_diagonal, own[1], beside_b)]]
    for group, name in zip(wide, ("a", "b")):
        for turn in range(1, half_cols):
            across = lambda h, i, y, k: (h, i, y, k ^ turn)
            group.append(send(group[0], across, f"wide_{name}_across_cores"))
    for mask in others:
        bit = 1 if mask ^ 1 in singles else mask & ~1 & -(mask & ~1)
        tall[mask][1] = swap_rows(tall[mask ^ bit][0 if bit == 1 else 1], bit, "forward_b")
        bit = 1 << (mask.bit_length() - 1)
        tall[mask][0] = swap_rows(tall[mask ^ bit][0], bit, "forward_a")

    def opposite(h, i, y, k, turn):
        return (1 - h, k * 2 + (i + turn) % 2, h, i // 2)

    def exchange(value, turn, cut):
        across = lambda h, i, y, k: opposite(h, i, y, k, turn) if h != y else None
        onward = lambda h, i, y, k: opposite(h, i, 1 - y, k, turn) if h == y else None
        pieces = []
        if cut > 0:
            pieces.append(send(value[:cut], across, f"near_{turn}_direct"))
        if cut < side:
            ahead = to_beside(value[cut:], False, f"near_{turn}_beside")
            pieces.append(send(ahead, onward, f"near_{turn}_ahead"))
        return pieces

    near, got, parts, far = {}, {}, [], []
    for step in STEPS:
        if isinstance(step, int):
            near[step], value = near_part(step)
            got[step] = exchange(value, step, CUTS[step] * side // 6)
        else:
            for m in range(0, half_rows, 2):
                if min(m // 2, 1) in step:
                    parts.append(([m, m + 1], far_product([m, m + 1])))
    for masks, part in parts:
        far.append(far_sum(masks, part))
    return final_sum(slots, [near[0], near[1]], far, [got[0], got[1]])


def solution(mesh):
    return jax.shard_map(
        functools.partial(shards, mesh.shape["row"], mesh.shape["col"]),
        mesh=mesh,
        in_specs=(P(None, AXES), P(None, AXES), P(), P("row", "col"), P(), P()),
        out_specs=P("row", "col"),
        check_vma=False,
    )
```

```python
import functools

import jax
import jax.numpy as jnp
from jax import lax
from jax.experimental import pallas as pl
from jax.experimental.pallas import tpu as pltpu
from jax.sharding import PartitionSpec as P

ORB = 128
NR = 16
AXES = ("row", "col")
VMEM_BYTES = 127 * 512 * 1024
EDGE_CHUNK = 256
BYTES_PER_US = 1_500_000
STEPS = ((0,), 1, 0, (1,))
CUTS = (6, 2)
PLAN = {
    'density_b_across_rows_2': ('raw_a_across_rows_1', 'raw_a_across_rows_2', 'raw_a_beside'),
    'far_2_3_across_cores': ('near_1_beside', 'near_1_direct'),
    'wide_b_across_cores': ('density_b_across_rows_1', 'density_b_across_rows_2'),
}


def taking(microseconds):
    return pl.CostEstimate(flops=0, bytes_accessed=int(microseconds * BYTES_PER_US), transcendentals=0)


def prepare_kernel(cells, chunks, atoms, atoms_total, edges, corner, coefficient, hits, embedding):
    count = edges.shape[1]
    size = count // chunks
    vec = edges[0:3, :]
    squared = vec[0:1] * vec[0:1] + vec[1:2] * vec[1:2] + vec[2:3] * vec[2:3]
    radius = jnp.sqrt(squared + 0.25)
    x, y, z = vec[0:1] / radius, vec[1:2] / radius, vec[2:3] / radius
    harmonics = jnp.concatenate(
        [jnp.ones_like(x), x, y, z, x * y, y * z, z * x, x * x - y * y, 3.0 * z * z - 1.0], axis=0
    )
    for k in range(NR):
        away = (radius - (1.0 + 0.3 * k)) / 0.5
        embedding[9 * k : 9 * k + 9, :] = jnp.exp(-(away * away)) * harmonics

    flipped = edges[...].T
    first, second = flipped[:, 3:4], flipped[:, 4:5]
    position = first * atoms_total + second
    position_row = edges[3:4, :] * atoms_total + edges[4:5, :]
    same = position == position_row
    coefficient[...] = lax.dot_general(
        same.astype(jnp.float32),
        embedding[...],
        (((1,), (1,)), ((), ())),
        precision=lax.Precision.HIGHEST,
        preferred_element_type=jnp.float32,
    ).astype(jnp.bfloat16)
    before = lax.broadcasted_iota(jnp.int32, (count, count), 1) < lax.broadcasted_iota(jnp.int32, (count, count), 0)
    repeated = jnp.max(jnp.where(same & before, 1.0, 0.0), axis=1, keepdims=True)

    mirrored = corner[2:3, :]
    row = first + mirrored * (second - first) - corner[0:1, :]
    col = second + mirrored * (first - second) - corner[1:2, :]
    limit = float(atoms)
    found = (row >= 0) & (row < limit) & (col >= 0) & (col < limit) & (corner[3:4, :] > 0) & (repeated < 0.5)
    found = jnp.where(found, 1.0, 0.0)
    lanes = lax.broadcasted_iota(jnp.int32, (1, ORB), 1).astype(jnp.float32)
    index = lax.broadcasted_iota(jnp.int32, (size, 1), 0).astype(jnp.float32)
    upto = lax.broadcasted_iota(jnp.int32, (size, size), 1) <= lax.broadcasted_iota(jnp.int32, (size, size), 0)
    upto = jnp.where(upto, 1.0, 0.0).astype(jnp.bfloat16)
    for chunk in range(chunks):
        part = slice(chunk * size, (chunk + 1) * size)
        here = found[part]
        place = jnp.dot(upto, here.astype(jnp.bfloat16), preferred_element_type=jnp.float32)
        code = (index * 2 + mirrored) * 4096 + row[part] * 64 + col[part]
        place = jnp.where(here > 0.5, place - 1.0, -1000.0)
        total = jnp.sum(here, axis=0, keepdims=True)
        for cell in range(cells):
            other = cells + cell
            direct = total[:, cell : cell + 1]
            at = jnp.where(place[:, cell : cell + 1] == lanes, code[:, cell : cell + 1], 0.0)
            at = at + jnp.where(place[:, other : other + 1] + direct == lanes, code[:, other : other + 1], 0.0)
            codes = jnp.sum(at, axis=0, keepdims=True)
            codes = jnp.where(lanes == ORB - 1, direct + total[:, other : other + 1], codes)
            hits[chunk, cell : cell + 1, :] = codes.astype(jnp.int32)


def cell_table(corner):
    cells = corner.shape[1]
    once = jnp.concatenate([corner, jnp.zeros((1, cells), jnp.int32), jnp.ones((1, cells), jnp.int32)])
    twice = jnp.concatenate([corner, jnp.ones((2, cells), jnp.int32)])
    table = jnp.concatenate([once, twice], axis=1).astype(jnp.float32)
    return jnp.pad(table, ((0, 4), (0, ORB - 2 * cells)))


def prepare(edges, table, cells, atoms, atoms_total):
    count = edges.shape[1]
    chunks = max(1, count // EDGE_CHUNK)
    return pl.pallas_call(
        functools.partial(prepare_kernel, cells, chunks, atoms, atoms_total),
        out_shape=[
            jax.ShapeDtypeStruct((count, 9 * NR), jnp.bfloat16),
            jax.ShapeDtypeStruct((chunks, cells, ORB), jnp.int32),
        ],
        scratch_shapes=[pltpu.VMEM((9 * NR, count), jnp.float32)],
        cost_estimate=taking(3),
        compiler_params=pltpu.CompilerParams(vmem_limit_bytes=VMEM_BYTES),
    )(edges, table)


def density_kernel(chunks, sources, unread, base, hits, scale, corner, coefficient, weight, *refs):
    cells = len(sources)
    refs = list(refs)
    raw = [[refs.pop(0) for _ in range(n)] for n in sources]
    refs = refs[unread:]
    out, (raw_in, total, ready, blocks, sems) = refs[:cells], refs[cells:]
    size = coefficient.shape[0] // chunks
    side = total.shape[0]
    wide = 8
    pitch = ORB + 8
    copies = []
    for n, refs_of in enumerate(raw):
        ways = [pltpu.make_async_copy(ref, raw_in.at[n], sems.at[0, n]) for ref in refs_of]
        copies.append(ways[0])
        if len(ways) == 1:
            ways[0].start()
        else:
            pl.when(scale[2] > 0.5)(ways[0].start)
            pl.when(scale[2] < 0.5)(ways[1].start)
    inverse = scale[1]

    def expand(chunk):
        def step(i, _):
            at = pl.multiple_of(i * (ORB * wide), ORB * wide)
            value = jnp.dot(
                coefficient[pl.ds(chunk * size, size), :],
                weight[:, pl.ds(at, ORB * wide)],
                preferred_element_type=jnp.float32,
            )
            for part in range(wide):
                blocks[pl.ds(i * wide + part, size, stride=pitch), :] = value[:, part * ORB : (part + 1) * ORB]
            return 0

        lax.fori_loop(0, ORB // wide, step, 0)

    if chunks == 1:
        expand(0)
    writes = []
    for n in range(cells):
        copies[n].wait()

        def spread(i, _):
            at = pl.ds(pl.multiple_of(i * ORB, ORB), ORB)
            total[at, :] = raw_in[n, at, :].astype(jnp.float32) * (-inverse)
            return 0

        lax.fori_loop(0, side // ORB, spread, 0)

        @pl.when(corner[0, base + n] == corner[1, base + n])
        def _():
            rows = lax.broadcasted_iota(jnp.int32, (ORB, ORB), 0)
            cols = lax.broadcasted_iota(jnp.int32, (ORB, ORB), 1)
            unit = jnp.where(rows == cols, scale[0], jnp.float32(0.0))
            for at in range(0, side, ORB):
                total[at : at + ORB, at : at + ORB] += unit

        for chunk in range(chunks):
            if chunks > 1:
                expand(chunk)

            def scatter(t, _):
                hit = hits[chunk, base + n, t]
                col = pl.multiple_of((hit % 64) * ORB, ORB)
                row = pl.multiple_of((hit // 64 % 64) * ORB, ORB)
                pair = hit // 4096
                spot = (pl.ds(row, ORB), pl.ds(col, ORB))
                block = blocks[pl.ds(pl.multiple_of(pair // 2 * pitch, 8), ORB), :] * inverse

                @pl.when(pair % 2 == 0)
                def _():
                    total[spot] = total[spot] - block

                @pl.when(pair % 2 == 1)
                def _():
                    total[spot] = total[spot] - block.T

                return 0

            lax.fori_loop(0, hits[chunk, base + n, ORB - 1], scatter, 0)

        def finish(i, _):
            at = pl.ds(pl.multiple_of(i * ORB, ORB), ORB)
            ready[n, at, :] = total[at, :].astype(jnp.bfloat16)
            return 0

        lax.fori_loop(0, side // ORB, finish, 0)
        writes.append(pltpu.make_async_copy(ready.at[n], out[n], sems.at[1, n]))
        writes[-1].start()
    for write in writes:
        write.wait()


def densities(raw, base, corner, hits, scale, coefficient, weight, sooner):
    cells = len(raw)
    sources = [len(refs) for refs in raw]
    raw = [ref for refs in raw for ref in refs]
    side = raw[0].shape[0]
    edges = coefficient.shape[0]
    chunks = max(1, edges // EDGE_CHUNK)
    any_spec = pl.BlockSpec(memory_space=pl.ANY)
    return pl.pallas_call(
        functools.partial(density_kernel, chunks, sources, len(sooner), base),
        out_shape=[jax.ShapeDtypeStruct((side, side), jnp.bfloat16)] * cells,
        in_specs=[pl.BlockSpec(memory_space=pltpu.SMEM)] * 3
        + [pl.BlockSpec(memory_space=pltpu.VMEM)] * 2
        + [any_spec] * (len(raw) + len(sooner)),
        out_specs=[any_spec] * cells,
        scratch_shapes=[
            pltpu.VMEM((cells, side, side), jnp.bfloat16),
            pltpu.VMEM((side, side), jnp.float32),
            pltpu.VMEM((cells, side, side), jnp.bfloat16),
            pltpu.VMEM((edges // chunks * (ORB + 8), ORB), jnp.float32),
            pltpu.SemaphoreType.DMA((2, cells)),
        ],
        cost_estimate=taking(6 + 2.5 * cells),
        compiler_params=pltpu.CompilerParams(vmem_limit_bytes=VMEM_BYTES),
    )(hits, scale, corner, coefficient, weight, *raw, *sooner)


def add_product(total, left, right, transposed, fresh):
    rows = total.shape[0]
    block = rows // 2
    contract = (((1,), (1,)), ((), ())) if transposed else (((1,), (0,)), ((), ()))
    for start in range(0, rows, block):
        at = pl.ds(start, block)
        value = lax.dot_general(left[at, :], right[...], contract, preferred_element_type=jnp.float32)
        total[at, :] = value if fresh else total[at, :] + value


def near_kernel(sides, sources, seeded, last, unread, source, *refs):
    count = len(sides)
    refs = list(refs)
    tall = [refs.pop(0) for _ in range(count)]
    wide = [[refs.pop(0) for _ in range(sources)] for _ in range(2)]
    seed = refs.pop(0) if seeded else None
    refs = refs[unread:]
    total = refs.pop(0)
    rounded = refs.pop(0) if last else None
    tall_in, wide_in, sems = refs
    waits = []
    for n in range(count):
        for s in range(sources):

            @pl.when(source[n] == s)
            def _():
                pltpu.make_async_copy(wide[sides[n]][s], wide_in.at[n], sems.at[n, 0]).start()

        here = [
            pltpu.make_async_copy(wide[sides[n]][0], wide_in.at[n], sems.at[n, 0]),
            pltpu.make_async_copy(tall[n], tall_in.at[n], sems.at[n, 1]),
        ]
        here[1].start()
        if seeded and n == 0:
            here.append(pltpu.make_async_copy(seed, total, sems.at[count, 0]))
            here[-1].start()
        waits.append(here)
    for n in range(count):
        for copy in waits[n]:
            copy.wait()
        add_product(total, wide_in.at[n], tall_in.at[n], False, n == 0 and not seeded)
    if last:
        rounded[...] = total[...].astype(jnp.bfloat16)


def near_share(source, tall, sides, wide, seed, last, sooner):
    cell = tall[0].shape
    sources = len(wide[0])
    count = len(tall)
    any_spec = pl.BlockSpec(memory_space=pl.ANY)
    operands = [source, *tall, *wide[0], *wide[1]]
    if seed is not None:
        operands.append(seed)
    operands += sooner
    shapes = [jax.ShapeDtypeStruct(cell, jnp.float32)]
    if last:
        shapes.append(jax.ShapeDtypeStruct(cell, jnp.bfloat16))
    return pl.pallas_call(
        functools.partial(near_kernel, sides, sources, seed is not None, last, len(sooner)),
        out_shape=shapes,
        in_specs=[pl.BlockSpec(memory_space=pltpu.SMEM)] + [any_spec] * (len(operands) - 1),
        out_specs=[pl.BlockSpec(memory_space=pltpu.VMEM)] * len(shapes),
        scratch_shapes=[
            pltpu.VMEM((count,) + cell, jnp.bfloat16),
            pltpu.VMEM((count,) + cell, jnp.bfloat16),
            pltpu.SemaphoreType.DMA((count + 1, 2)),
        ],
        cost_estimate=taking(2 + 2.5 * count),
        compiler_params=pltpu.CompilerParams(vmem_limit_bytes=VMEM_BYTES),
    )(*operands)


def far_kernel(count, unread, *refs):
    cells = refs[: 2 + 2 * count]
    out, cells_in, total, sems = refs[2 + 2 * count + unread :]
    copies = [pltpu.make_async_copy(ref, cells_in.at[n], sems.at[n]) for n, ref in enumerate(cells)]
    for copy in copies:
        copy.start()
    copies[0].wait()
    copies[1].wait()
    for m in range(count):
        for q in range(2):
            n = 2 + 2 * m + q
            copies[n].wait()
            add_product(total, cells_in.at[q], cells_in.at[n], True, q == 0)
        out[m] = total[...].astype(jnp.bfloat16)


def far_share(own, tall, sooner):
    cell = own[0].shape
    count = len(tall) // 2
    items = 2 + 2 * count
    any_spec = pl.BlockSpec(memory_space=pl.ANY)
    return pl.pallas_call(
        functools.partial(far_kernel, count, len(sooner)),
        out_shape=jax.ShapeDtypeStruct((count,) + cell, jnp.bfloat16),
        in_specs=[any_spec] * (items + len(sooner)),
        out_specs=pl.BlockSpec(memory_space=pltpu.VMEM),
        scratch_shapes=[
            pltpu.VMEM((items,) + cell, jnp.bfloat16),
            pltpu.VMEM(cell, jnp.float32),
            pltpu.SemaphoreType.DMA((items,)),
        ],
        cost_estimate=taking(3 + 3 * count),
        compiler_params=pltpu.CompilerParams(vmem_limit_bytes=VMEM_BYTES),
    )(*own, *tall, *sooner)


def final_kernel(parts, pieces, slot, *refs):
    refs = list(refs)
    near = [refs.pop(0) for _ in range(2)]
    far = [[refs.pop(0) for _ in range(n)] for n in parts]
    opposite = [[refs.pop(0) for _ in range(n)] for n in pieces]
    out = refs.pop(0)
    turn = pl.program_id(0)
    block = 128
    for q in range(2):

        @pl.when(turn == q)
        def _():
            start = 0
            for piece in opposite[q]:
                rows = piece.shape[0]

                def step(n, _):
                    at = pl.ds(pl.multiple_of(n * block, block), block)
                    to = pl.ds(start, rows)
                    value = near[q][at, to]
                    for share in far:
                        part = share[q][0, at, to] if len(share) == 2 else share[0][q, at, to]
                        value = value + part.astype(jnp.float32)
                    out[at, to] = value + piece[:, at].astype(jnp.float32).T
                    return 0

                lax.fori_loop(0, out.shape[0] // block, step, 0)
                start += rows


def final_sum(slot, near, far, opposite):
    side = near[0].shape[0]
    operands = [*near, *[part for share in far for part in share], *opposite[0], *opposite[1]]
    return pl.pallas_call(
        functools.partial(final_kernel, [len(share) for share in far], [len(pieces) for pieces in opposite]),
        out_shape=jax.ShapeDtypeStruct((side, 2 * side), jnp.float32),
        grid_spec=pltpu.PrefetchScalarGridSpec(
            num_scalar_prefetch=1,
            grid=(2,),
            in_specs=[pl.BlockSpec(o.shape, lambda t, s, n=len(o.shape): (0,) * n) for o in operands],
            out_specs=pl.BlockSpec((side, side), lambda t, s: (0, s[t])),
        ),
        cost_estimate=taking(9),
        compiler_params=pltpu.CompilerParams(vmem_limit_bytes=VMEM_BYTES),
    )(slot, *operands)


def after(value, *earlier):
    return lax.optimization_barrier((value, *earlier))[0] if earlier else value


def shards(row_size, col_size, edge_vec, edge_atoms, block_weight, base, lower_bound, upper_bound):
    devices = row_size * col_size
    half_rows = row_size // 2
    half_cols = col_size // 2
    side = base.shape[0]
    atoms = side // ORB
    row = lax.axis_index("row")
    col = lax.axis_index("col")
    row_half, row_in = row // half_rows, row % half_rows
    col_half, col_in = col // half_cols, col % half_cols
    on_diagonal = row_half == col_half
    slots = jnp.stack([row_in % 2, 1 - row_in % 2]).astype(jnp.int32)

    def moves(where):
        pairs = []
        for r in range(row_size):
            for c in range(col_size):
                to = where(r // half_rows, r % half_rows, c // half_cols, c % half_cols)
                if to is not None:
                    h, i, y, k = to
                    pairs.append((r * col_size + c, (h * half_rows + i) * col_size + y * half_cols + k))
        return pairs

    made = {}

    def waits(what):
        return [made[name] for name in PLAN.get(what, ()) if name in made]

    def send(value, where, what):
        with jax.named_scope(what):
            made[what] = lax.ppermute(after(value, *waits(what)), AXES, moves(where))
        return made[what]

    def swap_rows(value, bit, what):
        return send(value, lambda h, i, y, k: (h, i ^ bit, y, k), f"{what}_across_rows_{bit}")

    def to_beside(value, from_diagonal, what):
        return send(value, lambda h, i, y, k: (h, i, 1 - y, k) if (h == y) == from_diagonal else None, what)

    raw = [lax.dynamic_slice(base, (0, slots[q] * side), (side, side)) for q in range(2)]
    singles = [1 << b for b in range(half_rows.bit_length() - 1)]
    others = [m for m in range(1, half_rows) if m & (m - 1)]

    span = upper_bound[0] - lower_bound[0]
    scale = jnp.stack([upper_bound[0] / span, 1.0 / span, on_diagonal.astype(jnp.float32)])

    def tall_corner(mask, q):
        return row_half * half_rows + (row_in ^ mask), 2 * col + slots[q]

    corners = [tall_corner(0, q) for q in range(2)] + [tall_corner(m, 0) for m in singles]
    corners += [(row, row_half * half_rows + 2 * col_in + slots[0])]
    corner = jnp.stack([jnp.stack([c[n] for c in corners]) for n in range(2)]).astype(jnp.int32) * atoms
    table = cell_table(corner)

    edges = jnp.concatenate(
        [edge_vec, edge_atoms.astype(jnp.float32), jnp.zeros((3, edge_vec.shape[1]), jnp.float32)], axis=0
    )
    raw_a = {0: raw[0]}

    def double(value, bit):
        arrived = lax.ppermute(value, AXES, [(d, d ^ bit) for d in range(devices)])
        return jnp.concatenate([value, arrived], axis=1)

    bit = devices // 2
    while bit > col_size:
        edges = double(edges, bit)
        bit //= 2
        edges = after(edges, *((raw[0], raw[1]) if bit == col_size else (table, scale, corner)))
    for mask in singles[1:]:
        raw_a[mask] = swap_rows(after(raw[0], edges), mask, "raw_a")
    edges = double(edges, col_size)
    raw_a[1] = swap_rows(after(raw[1], edges), 1, "raw_a")
    bit = col_size // 2
    while bit >= half_cols:
        edges = double(edges, bit)
        bit //= 2
    beside_a = to_beside(after(raw[0], edges), True, "raw_a_beside")
    while bit:
        edges = double(edges, bit)
        bit //= 2

    done = []
    sums = []
    beside = []

    coefficient, hits = prepare(edges, table, len(corners), atoms, atoms * row_size)

    def density(cells, at):
        what = f"density_{at}"
        with jax.named_scope(what):
            got = densities(cells, at, corner, hits, scale, coefficient, block_weight, [*done[-1:], *waits(what)])
        done.append(got[0])
        return got

    tall = {mask: [None, None] for mask in range(half_rows)}
    def near_part(q):
        what = f"near_{q}"
        place = after((row_in // 2) ^ col_in, *waits(what + "_source"))
        source = jnp.stack([place ^ (m // 2) for m in range(half_rows)]).astype(jnp.int32)
        sides = tuple(m % 2 for m in range(half_rows))
        with jax.named_scope(what):
            got = near_share(source, [tall[m][q] for m in tall], sides, wide, None, True, [*done[-1:], *waits(what)])
        done.append(got[0])
        made[what] = got[1]
        return got

    def far_product(masks):
        what = "far_" + "_".join(map(str, masks))
        with jax.named_scope(what):
            part = far_share(own, [tall[m][q] for m in masks for q in range(2)], [*done[-1:], *waits(what)])
        done.append(part)
        made[what] = part
        return part

    def far_sum(masks, part):
        what = "far_" + "_".join(map(str, masks))
        owner = lambda i: (i // 2) ^ (masks[0] // 2)
        summed = part.astype(jnp.float32)
        for turn in range(1, half_cols):
            arrived = send(
                part,
                lambda h, i, y, k: (h, i, y, owner(i)) if h != y and k == owner(i) ^ turn else None,
                what + "_across_cores",
            )
            summed = summed + arrived.astype(jnp.float32)
        across = lambda h, i, y, k: (h, i, 1 - y, k) if h != y and k == owner(i) else None
        summed = summed.astype(jnp.bfloat16)
        if masks[0] == 0:
            return [send(summed, across, f"{what}_beside")]
        return [send(summed[n : n + 1], across, f"{what}_beside_{n}") for n in range(2)]

    tall[0] = density([[cell] for cell in raw], 0)
    own = tall[0]
    tall[1][1] = swap_rows(own[0], 1, "density_b")
    beside_b = to_beside(own[1], True, "density_b_beside")
    for mask in singles[1:]:
        tall[mask][1] = swap_rows(own[1], mask, "density_b")
    got = density([[raw_a[m]] for m in singles] + [[raw[0], beside_a]], 2)
    for mask, value in zip(singles, got):
        tall[mask][0] = value
    wide = [[got[len(singles)]], [jnp.where(on_diagonal, own[1], beside_b)]]
    for group, name in zip(wide, ("a", "b")):
        for turn in range(1, half_cols):
            across = lambda h, i, y, k: (h, i, y, k ^ turn)
            group.append(send(group[0], across, f"wide_{name}_across_cores"))
    for mask in others:
        bit = 1 if mask ^ 1 in singles else mask & ~1 & -(mask & ~1)
        tall[mask][1] = swap_rows(tall[mask ^ bit][0 if bit == 1 else 1], bit, "forward_b")
        bit = 1 << (mask.bit_length() - 1)
        tall[mask][0] = swap_rows(tall[mask ^ bit][0], bit, "forward_a")

    def opposite(h, i, y, k, turn):
        return (1 - h, k * 2 + (i + turn) % 2, h, i // 2)

    def exchange(value, turn, cut):
        across = lambda h, i, y, k: opposite(h, i, y, k, turn) if h != y else None
        onward = lambda h, i, y, k: opposite(h, i, 1 - y, k, turn) if h == y else None
        pieces = []
        if cut > 0:
            pieces.append(send(value[:cut], across, f"near_{turn}_direct"))
        if cut < side:
            ahead = to_beside(value[cut:], False, f"near_{turn}_beside")
            pieces.append(send(ahead, onward, f"near_{turn}_ahead"))
        return pieces

    near, got, parts, far = {}, {}, [], []
    for step in STEPS:
        if isinstance(step, int):
            near[step], value = near_part(step)
            got[step] = exchange(value, step, CUTS[step] * side // 6)
        else:
            for m in range(0, half_rows, 2):
                if min(m // 2, 1) in step:
                    parts.append(([m, m + 1], far_product([m, m + 1])))
    for masks, part in parts:
        far.append(far_sum(masks, part))
    return final_sum(slots, [near[0], near[1]], far, [got[0], got[1]])


def solution(mesh):
    return jax.shard_map(
        functools.partial(shards, mesh.shape["row"], mesh.shape["col"]),
        mesh=mesh,
        in_specs=(P(None, AXES), P(None, AXES), P(), P("row", "col"), P(), P()),
        out_specs=P("row", "col"),
        check_vma=False,
    )
```

```python
import functools

import jax
import jax.numpy as jnp
from jax import lax
from jax.experimental import pallas as pl
from jax.experimental.pallas import tpu as pltpu
from jax.sharding import PartitionSpec as P

ORB = 128
NR = 16
AXES = ("row", "col")
VMEM_BYTES = 127 * 512 * 1024
EDGE_CHUNK = 256
BYTES_PER_US = 1_500_000
STEPS = ((0,), 1, 0, (1,))
CUTS = (6, 2)
PLAN = {
    'density_b_across_rows_2': ('raw_a_across_rows_1', 'raw_a_across_rows_2', 'raw_a_beside'),
    'far_2_3_across_cores': ('near_1_beside', 'near_1_direct'),
    'wide_b_across_cores': ('density_b_across_rows_1', 'density_b_across_rows_2'),
}


def taking(microseconds):
    return pl.CostEstimate(flops=0, bytes_accessed=int(microseconds * BYTES_PER_US), transcendentals=0)


def prepare_kernel(cells, chunks, atoms, atoms_total, edges, corner, coefficient, hits, embedding):
    count = edges.shape[1]
    size = count // chunks
    vec = edges[0:3, :]
    squared = vec[0:1] * vec[0:1] + vec[1:2] * vec[1:2] + vec[2:3] * vec[2:3]
    radius = jnp.sqrt(squared + 0.25)
    x, y, z = vec[0:1] / radius, vec[1:2] / radius, vec[2:3] / radius
    harmonics = jnp.concatenate(
        [jnp.ones_like(x), x, y, z, x * y, y * z, z * x, x * x - y * y, 3.0 * z * z - 1.0], axis=0
    )
    for k in range(NR):
        away = (radius - (1.0 + 0.3 * k)) / 0.5
        embedding[9 * k : 9 * k + 9, :] = jnp.exp(-(away * away)) * harmonics

    flipped = edges[...].T
    first, second = flipped[:, 3:4], flipped[:, 4:5]
    position = first * atoms_total + second
    position_row = edges[3:4, :] * atoms_total + edges[4:5, :]
    same = position == position_row
    coefficient[...] = lax.dot_general(
        same.astype(jnp.float32),
        embedding[...],
        (((1,), (1,)), ((), ())),
        precision=lax.Precision.HIGHEST,
        preferred_element_type=jnp.float32,
    ).astype(jnp.bfloat16)
    before = lax.broadcasted_iota(jnp.int32, (count, count), 1) < lax.broadcasted_iota(jnp.int32, (count, count), 0)
    repeated = jnp.max(jnp.where(same & before, 1.0, 0.0), axis=1, keepdims=True)

    mirrored = corner[2:3, :]
    row = first + mirrored * (second - first) - corner[0:1, :]
    col = second + mirrored * (first - second) - corner[1:2, :]
    limit = float(atoms)
    found = (row >= 0) & (row < limit) & (col >= 0) & (col < limit) & (corner[3:4, :] > 0) & (repeated < 0.5)
    found = jnp.where(found, 1.0, 0.0)
    lanes = lax.broadcasted_iota(jnp.int32, (1, ORB), 1).astype(jnp.float32)
    index = lax.broadcasted_iota(jnp.int32, (size, 1), 0).astype(jnp.float32)
    upto = lax.broadcasted_iota(jnp.int32, (size, size), 1) <= lax.broadcasted_iota(jnp.int32, (size, size), 0)
    upto = jnp.where(upto, 1.0, 0.0).astype(jnp.bfloat16)
    for chunk in range(chunks):
        part = slice(chunk * size, (chunk + 1) * size)
        here = found[part]
        place = jnp.dot(upto, here.astype(jnp.bfloat16), preferred_element_type=jnp.float32)
        code = (index * 2 + mirrored) * 4096 + row[part] * 64 + col[part]
        place = jnp.where(here > 0.5, place - 1.0, -1000.0)
        total = jnp.sum(here, axis=0, keepdims=True)
        for cell in range(cells):
            other = cells + cell
            direct = total[:, cell : cell + 1]
            at = jnp.where(place[:, cell : cell + 1] == lanes, code[:, cell : cell + 1], 0.0)
            at = at + jnp.where(place[:, other : other + 1] + direct == lanes, code[:, other : other + 1], 0.0)
            codes = jnp.sum(at, axis=0, keepdims=True)
            codes = jnp.where(lanes == ORB - 1, direct + total[:, other : other + 1], codes)
            hits[chunk, cell : cell + 1, :] = codes.astype(jnp.int32)


def cell_table(corner):
    cells = corner.shape[1]
    once = jnp.concatenate([corner, jnp.zeros((1, cells), jnp.int32), jnp.ones((1, cells), jnp.int32)])
    twice = jnp.concatenate([corner, jnp.ones((2, cells), jnp.int32)])
    table = jnp.concatenate([once, twice], axis=1).astype(jnp.float32)
    return jnp.pad(table, ((0, 4), (0, ORB - 2 * cells)))


def prepare(edges, table, cells, atoms, atoms_total):
    count = edges.shape[1]
    chunks = max(1, count // EDGE_CHUNK)
    return pl.pallas_call(
        functools.partial(prepare_kernel, cells, chunks, atoms, atoms_total),
        out_shape=[
            jax.ShapeDtypeStruct((count, 9 * NR), jnp.bfloat16),
            jax.ShapeDtypeStruct((chunks, cells, ORB), jnp.int32),
        ],
        scratch_shapes=[pltpu.VMEM((9 * NR, count), jnp.float32)],
        cost_estimate=taking(3),
        compiler_params=pltpu.CompilerParams(vmem_limit_bytes=VMEM_BYTES),
    )(edges, table)


def density_kernel(chunks, sources, unread, base, hits, scale, corner, coefficient, weight, *refs):
    cells = len(sources)
    refs = list(refs)
    raw = [[refs.pop(0) for _ in range(n)] for n in sources]
    refs = refs[unread:]
    out, (raw_in, total, ready, blocks, sems) = refs[:cells], refs[cells:]
    size = coefficient.shape[0] // chunks
    side = total.shape[0]
    wide = 8
    pitch = ORB + 8
    copies = []
    for n, refs_of in enumerate(raw):
        ways = [pltpu.make_async_copy(ref, raw_in.at[n], sems.at[0, n]) for ref in refs_of]
        copies.append(ways[0])
        if len(ways) == 1:
            ways[0].start()
        else:
            pl.when(scale[2] > 0.5)(ways[0].start)
            pl.when(scale[2] < 0.5)(ways[1].start)
    inverse = scale[1]

    def expand(chunk):
        def step(i, _):
            at = pl.multiple_of(i * (ORB * wide), ORB * wide)
            value = jnp.dot(
                coefficient[pl.ds(chunk * size, size), :],
                weight[:, pl.ds(at, ORB * wide)],
                preferred_element_type=jnp.float32,
            )
            for part in range(wide):
                blocks[pl.ds(i * wide + part, size, stride=pitch), :] = value[:, part * ORB : (part + 1) * ORB]
            return 0

        lax.fori_loop(0, ORB // wide, step, 0)

    if chunks == 1:
        expand(0)
    writes = []
    for n in range(cells):
        copies[n].wait()

        def spread(i, _):
            at = pl.ds(pl.multiple_of(i * ORB, ORB), ORB)
            total[at, :] = raw_in[n, at, :].astype(jnp.float32) * (-inverse)
            return 0

        lax.fori_loop(0, side // ORB, spread, 0)

        @pl.when(corner[0, base + n] == corner[1, base + n])
        def _():
            rows = lax.broadcasted_iota(jnp.int32, (ORB, ORB), 0)
            cols = lax.broadcasted_iota(jnp.int32, (ORB, ORB), 1)
            unit = jnp.where(rows == cols, scale[0], jnp.float32(0.0))
            for at in range(0, side, ORB):
                total[at : at + ORB, at : at + ORB] += unit

        for chunk in range(chunks):
            if chunks > 1:
                expand(chunk)

            def scatter(t, _):
                hit = hits[chunk, base + n, t]
                col = pl.multiple_of((hit % 64) * ORB, ORB)
                row = pl.multiple_of((hit // 64 % 64) * ORB, ORB)
                pair = hit // 4096
                spot = (pl.ds(row, ORB), pl.ds(col, ORB))
                block = blocks[pl.ds(pl.multiple_of(pair // 2 * pitch, 8), ORB), :] * inverse

                @pl.when(pair % 2 == 0)
                def _():
                    total[spot] = total[spot] - block

                @pl.when(pair % 2 == 1)
                def _():
                    total[spot] = total[spot] - block.T

                return 0

            lax.fori_loop(0, hits[chunk, base + n, ORB - 1], scatter, 0)

        def finish(i, _):
            at = pl.ds(pl.multiple_of(i * ORB, ORB), ORB)
            ready[n, at, :] = total[at, :].astype(jnp.bfloat16)
            return 0

        lax.fori_loop(0, side // ORB, finish, 0)
        writes.append(pltpu.make_async_copy(ready.at[n], out[n], sems.at[1, n]))
        writes[-1].start()
    for write in writes:
        write.wait()


def densities(raw, base, corner, hits, scale, coefficient, weight, sooner):
    cells = len(raw)
    sources = [len(refs) for refs in raw]
    raw = [ref for refs in raw for ref in refs]
    side = raw[0].shape[0]
    edges = coefficient.shape[0]
    chunks = max(1, edges // EDGE_CHUNK)
    any_spec = pl.BlockSpec(memory_space=pl.ANY)
    return pl.pallas_call(
        functools.partial(density_kernel, chunks, sources, len(sooner), base),
        out_shape=[jax.ShapeDtypeStruct((side, side), jnp.bfloat16)] * cells,
        in_specs=[pl.BlockSpec(memory_space=pltpu.SMEM)] * 3
        + [pl.BlockSpec(memory_space=pltpu.VMEM)] * 2
        + [any_spec] * (len(raw) + len(sooner)),
        out_specs=[any_spec] * cells,
        scratch_shapes=[
            pltpu.VMEM((cells, side, side), jnp.bfloat16),
            pltpu.VMEM((side, side), jnp.float32),
            pltpu.VMEM((cells, side, side), jnp.bfloat16),
            pltpu.VMEM((edges // chunks * (ORB + 8), ORB), jnp.float32),
            pltpu.SemaphoreType.DMA((2, cells)),
        ],
        cost_estimate=taking(6 + 2.5 * cells),
        compiler_params=pltpu.CompilerParams(vmem_limit_bytes=VMEM_BYTES),
    )(hits, scale, corner, coefficient, weight, *raw, *sooner)


def add_product(total, left, right, transposed, fresh):
    rows = total.shape[0]
    block = rows // 2
    contract = (((1,), (1,)), ((), ())) if transposed else (((1,), (0,)), ((), ()))
    for start in range(0, rows, block):
        at = pl.ds(start, block)
        value = lax.dot_general(left[at, :], right[...], contract, preferred_element_type=jnp.float32)
        total[at, :] = value if fresh else total[at, :] + value


def near_kernel(sides, sources, seeded, last, unread, source, *refs):
    count = len(sides)
    refs = list(refs)
    tall = [refs.pop(0) for _ in range(count)]
    wide = [[refs.pop(0) for _ in range(sources)] for _ in range(2)]
    seed = refs.pop(0) if seeded else None
    refs = refs[unread:]
    total = refs.pop(0)
    rounded = refs.pop(0) if last else None
    tall_in, wide_in, sems = refs
    waits = []
    for n in range(count):
        for s in range(sources):

            @pl.when(source[n] == s)
            def _():
                pltpu.make_async_copy(wide[sides[n]][s], wide_in.at[n], sems.at[n, 0]).start()

        here = [
            pltpu.make_async_copy(wide[sides[n]][0], wide_in.at[n], sems.at[n, 0]),
            pltpu.make_async_copy(tall[n], tall_in.at[n], sems.at[n, 1]),
        ]
        here[1].start()
        if seeded and n == 0:
            here.append(pltpu.make_async_copy(seed, total, sems.at[count, 0]))
            here[-1].start()
        waits.append(here)
    for n in range(count):
        for copy in waits[n]:
            copy.wait()
        add_product(total, wide_in.at[n], tall_in.at[n], False, n == 0 and not seeded)
    if last:
        rounded[...] = total[...].astype(jnp.bfloat16)


def near_share(source, tall, sides, wide, seed, last, sooner):
    cell = tall[0].shape
    sources = len(wide[0])
    count = len(tall)
    any_spec = pl.BlockSpec(memory_space=pl.ANY)
    operands = [source, *tall, *wide[0], *wide[1]]
    if seed is not None:
        operands.append(seed)
    operands += sooner
    shapes = [jax.ShapeDtypeStruct(cell, jnp.float32)]
    if last:
        shapes.append(jax.ShapeDtypeStruct(cell, jnp.bfloat16))
    return pl.pallas_call(
        functools.partial(near_kernel, sides, sources, seed is not None, last, len(sooner)),
        out_shape=shapes,
        in_specs=[pl.BlockSpec(memory_space=pltpu.SMEM)] + [any_spec] * (len(operands) - 1),
        out_specs=[pl.BlockSpec(memory_space=pltpu.VMEM)] * len(shapes),
        scratch_shapes=[
            pltpu.VMEM((count,) + cell, jnp.bfloat16),
            pltpu.VMEM((count,) + cell, jnp.bfloat16),
            pltpu.SemaphoreType.DMA((count + 1, 2)),
        ],
        cost_estimate=taking(2 + 2.5 * count),
        compiler_params=pltpu.CompilerParams(vmem_limit_bytes=VMEM_BYTES),
    )(*operands)


def far_kernel(count, unread, *refs):
    cells = refs[: 2 + 2 * count]
    out, cells_in, total, sems = refs[2 + 2 * count + unread :]
    copies = [pltpu.make_async_copy(ref, cells_in.at[n], sems.at[n]) for n, ref in enumerate(cells)]
    for copy in copies:
        copy.start()
    copies[0].wait()
    copies[1].wait()
    for m in range(count):
        for q in range(2):
            n = 2 + 2 * m + q
            copies[n].wait()
            add_product(total, cells_in.at[q], cells_in.at[n], True, q == 0)
        out[m] = total[...].astype(jnp.bfloat16)


def far_share(own, tall, sooner):
    cell = own[0].shape
    count = len(tall) // 2
    items = 2 + 2 * count
    any_spec = pl.BlockSpec(memory_space=pl.ANY)
    return pl.pallas_call(
        functools.partial(far_kernel, count, len(sooner)),
        out_shape=jax.ShapeDtypeStruct((count,) + cell, jnp.bfloat16),
        in_specs=[any_spec] * (items + len(sooner)),
        out_specs=pl.BlockSpec(memory_space=pltpu.VMEM),
        scratch_shapes=[
            pltpu.VMEM((items,) + cell, jnp.bfloat16),
            pltpu.VMEM(cell, jnp.float32),
            pltpu.SemaphoreType.DMA((items,)),
        ],
        cost_estimate=taking(3 + 3 * count),
        compiler_params=pltpu.CompilerParams(vmem_limit_bytes=VMEM_BYTES),
    )(*own, *tall, *sooner)


def final_kernel(parts, pieces, slot, *refs):
    refs = list(refs)
    near = [refs.pop(0) for _ in range(2)]
    far = [[refs.pop(0) for _ in range(n)] for n in parts]
    opposite = [[refs.pop(0) for _ in range(n)] for n in pieces]
    out, near_in, far_in, opposite_in, sems = refs
    turn = pl.program_id(0)
    block = 128
    groups = len(far)
    copies = []
    for q in range(2):
        here = [pltpu.make_async_copy(near[q], near_in.at[q], sems.at[q, 0])]
        for n, share in enumerate(far):
            part = share[q].at[0] if len(share) == 2 else share[0].at[q]
            here.append(pltpu.make_async_copy(part, far_in.at[q, n], sems.at[q, 1 + n]))
        at = 0
        for n, piece in enumerate(opposite[q]):
            to = opposite_in.at[q, pl.ds(at, piece.shape[0])]
            here.append(pltpu.make_async_copy(piece, to, sems.at[q, 1 + groups + n]))
            at += piece.shape[0]
        copies.append(here)

    @pl.when(turn == 0)
    def _():
        for here in copies:
            for copy in here:
                copy.start()

    for q in range(2):

        @pl.when(turn == q)
        def _():
            for copy in copies[q]:
                copy.wait()

            def step(n, _):
                at = pl.ds(pl.multiple_of(n * block, block), block)
                value = near_in[q, at, :]
                for n in range(groups):
                    value = value + far_in[q, n, at, :].astype(jnp.float32)
                out[at, :] = value + opposite_in[q, :, at].astype(jnp.float32).T
                return 0

            lax.fori_loop(0, out.shape[0] // block, step, 0)


def final_sum(slot, near, far, opposite):
    side = near[0].shape[0]
    groups = len(far)
    operands = [*near, *[part for share in far for part in share], *opposite[0], *opposite[1]]
    return pl.pallas_call(
        functools.partial(final_kernel, [len(share) for share in far], [len(pieces) for pieces in opposite]),
        out_shape=jax.ShapeDtypeStruct((side, 2 * side), jnp.float32),
        grid_spec=pltpu.PrefetchScalarGridSpec(
            num_scalar_prefetch=1,
            grid=(2,),
            in_specs=[pl.BlockSpec(memory_space=pl.ANY)] * len(operands),
            out_specs=pl.BlockSpec((side, side), lambda t, s: (0, s[t])),
            scratch_shapes=[
                pltpu.VMEM((2, side, side), jnp.float32),
                pltpu.VMEM((2, groups, side, side), jnp.bfloat16),
                pltpu.VMEM((2, side, side), jnp.bfloat16),
                pltpu.SemaphoreType.DMA((2, groups + 3)),
            ],
        ),
        cost_estimate=taking(9),
        compiler_params=pltpu.CompilerParams(vmem_limit_bytes=VMEM_BYTES),
    )(slot, *operands)


def after(value, *earlier):
    return lax.optimization_barrier((value, *earlier))[0] if earlier else value


def shards(row_size, col_size, edge_vec, edge_atoms, block_weight, base, lower_bound, upper_bound):
    devices = row_size * col_size
    half_rows = row_size // 2
    half_cols = col_size // 2
    side = base.shape[0]
    atoms = side // ORB
    row = lax.axis_index("row")
    col = lax.axis_index("col")
    row_half, row_in = row // half_rows, row % half_rows
    col_half, col_in = col // half_cols, col % half_cols
    on_diagonal = row_half == col_half
    slots = jnp.stack([row_in % 2, 1 - row_in % 2]).astype(jnp.int32)

    def moves(where):
        pairs = []
        for r in range(row_size):
            for c in range(col_size):
                to = where(r // half_rows, r % half_rows, c // half_cols, c % half_cols)
                if to is not None:
                    h, i, y, k = to
                    pairs.append((r * col_size + c, (h * half_rows + i) * col_size + y * half_cols + k))
        return pairs

    made = {}

    def waits(what):
        return [made[name] for name in PLAN.get(what, ()) if name in made]

    def send(value, where, what):
        with jax.named_scope(what):
            made[what] = lax.ppermute(after(value, *waits(what)), AXES, moves(where))
        return made[what]

    def swap_rows(value, bit, what):
        return send(value, lambda h, i, y, k: (h, i ^ bit, y, k), f"{what}_across_rows_{bit}")

    def to_beside(value, from_diagonal, what):
        return send(value, lambda h, i, y, k: (h, i, 1 - y, k) if (h == y) == from_diagonal else None, what)

    raw = [lax.dynamic_slice(base, (0, slots[q] * side), (side, side)) for q in range(2)]
    singles = [1 << b for b in range(half_rows.bit_length() - 1)]
    others = [m for m in range(1, half_rows) if m & (m - 1)]

    span = upper_bound[0] - lower_bound[0]
    scale = jnp.stack([upper_bound[0] / span, 1.0 / span, on_diagonal.astype(jnp.float32)])

    def tall_corner(mask, q):
        return row_half * half_rows + (row_in ^ mask), 2 * col + slots[q]

    corners = [tall_corner(0, q) for q in range(2)] + [tall_corner(m, 0) for m in singles]
    corners += [(row, row_half * half_rows + 2 * col_in + slots[0])]
    corner = jnp.stack([jnp.stack([c[n] for c in corners]) for n in range(2)]).astype(jnp.int32) * atoms
    table = cell_table(corner)

    edges = jnp.concatenate(
        [edge_vec, edge_atoms.astype(jnp.float32), jnp.zeros((3, edge_vec.shape[1]), jnp.float32)], axis=0
    )
    raw_a = {0: raw[0]}

    def double(value, bit):
        arrived = lax.ppermute(value, AXES, [(d, d ^ bit) for d in range(devices)])
        return jnp.concatenate([value, arrived], axis=1)

    bit = devices // 2
    while bit > col_size:
        edges = double(edges, bit)
        bit //= 2
        edges = after(edges, *((raw[0], raw[1]) if bit == col_size else (table, scale, corner)))
    for mask in singles[1:]:
        raw_a[mask] = swap_rows(after(raw[0], edges), mask, "raw_a")
    edges = double(edges, col_size)
    raw_a[1] = swap_rows(after(raw[1], edges), 1, "raw_a")
    bit = col_size // 2
    while bit >= half_cols:
        edges = double(edges, bit)
        bit //= 2
    beside_a = to_beside(after(raw[0], edges), True, "raw_a_beside")
    while bit:
        edges = double(edges, bit)
        bit //= 2

    done = []
    sums = []
    beside = []

    coefficient, hits = prepare(edges, table, len(corners), atoms, atoms * row_size)

    def density(cells, at):
        what = f"density_{at}"
        with jax.named_scope(what):
            got = densities(cells, at, corner, hits, scale, coefficient, block_weight, [*done[-1:], *waits(what)])
        done.append(got[0])
        return got

    tall = {mask: [None, None] for mask in range(half_rows)}
    def near_part(q):
        what = f"near_{q}"
        place = after((row_in // 2) ^ col_in, *waits(what + "_source"))
        source = jnp.stack([place ^ (m // 2) for m in range(half_rows)]).astype(jnp.int32)
        sides = tuple(m % 2 for m in range(half_rows))
        with jax.named_scope(what):
            got = near_share(source, [tall[m][q] for m in tall], sides, wide, None, True, [*done[-1:], *waits(what)])
        done.append(got[0])
        made[what] = got[1]
        return got

    def far_product(masks):
        what = "far_" + "_".join(map(str, masks))
        with jax.named_scope(what):
            part = far_share(own, [tall[m][q] for m in masks for q in range(2)], [*done[-1:], *waits(what)])
        done.append(part)
        made[what] = part
        return part

    def far_sum(masks, part):
        what = "far_" + "_".join(map(str, masks))
        owner = lambda i: (i // 2) ^ (masks[0] // 2)
        summed = part.astype(jnp.float32)
        for turn in range(1, half_cols):
            arrived = send(
                part,
                lambda h, i, y, k: (h, i, y, owner(i)) if h != y and k == owner(i) ^ turn else None,
                what + "_across_cores",
            )
            summed = summed + arrived.astype(jnp.float32)
        across = lambda h, i, y, k: (h, i, 1 - y, k) if h != y and k == owner(i) else None
        summed = summed.astype(jnp.bfloat16)
        if masks[0] == 0:
            return [send(summed, across, f"{what}_beside")]
        return [send(summed[n : n + 1], across, f"{what}_beside_{n}") for n in range(2)]

    tall[0] = density([[cell] for cell in raw], 0)
    own = tall[0]
    tall[1][1] = swap_rows(own[0], 1, "density_b")
    beside_b = to_beside(own[1], True, "density_b_beside")
    for mask in singles[1:]:
        tall[mask][1] = swap_rows(own[1], mask, "density_b")
    got = density([[raw_a[m]] for m in singles] + [[raw[0], beside_a]], 2)
    for mask, value in zip(singles, got):
        tall[mask][0] = value
    wide = [[got[len(singles)]], [jnp.where(on_diagonal, own[1], beside_b)]]
    for group, name in zip(wide, ("a", "b")):
        for turn in range(1, half_cols):
            across = lambda h, i, y, k: (h, i, y, k ^ turn)
            group.append(send(group[0], across, f"wide_{name}_across_cores"))
    for mask in others:
        bit = 1 if mask ^ 1 in singles else mask & ~1 & -(mask & ~1)
        tall[mask][1] = swap_rows(tall[mask ^ bit][0 if bit == 1 else 1], bit, "forward_b")
        bit = 1 << (mask.bit_length() - 1)
        tall[mask][0] = swap_rows(tall[mask ^ bit][0], bit, "forward_a")

    def opposite(h, i, y, k, turn):
        return (1 - h, k * 2 + (i + turn) % 2, h, i // 2)

    def exchange(value, turn, cut):
        across = lambda h, i, y, k: opposite(h, i, y, k, turn) if h != y else None
        onward = lambda h, i, y, k: opposite(h, i, 1 - y, k, turn) if h == y else None
        pieces = []
        if cut > 0:
            pieces.append(send(value[:cut], across, f"near_{turn}_direct"))
        if cut < side:
            ahead = to_beside(value[cut:], False, f"near_{turn}_beside")
            pieces.append(send(ahead, onward, f"near_{turn}_ahead"))
        return pieces

    near, got, parts, far = {}, {}, [], []
    for step in STEPS:
        if isinstance(step, int):
            near[step], value = near_part(step)
            got[step] = exchange(value, step, CUTS[step] * side // 6)
        else:
            for m in range(0, half_rows, 2):
                if min(m // 2, 1) in step:
                    parts.append(([m, m + 1], far_product([m, m + 1])))
    for masks, part in parts:
        far.append(far_sum(masks, part))
    return final_sum(slots, [near[0], near[1]], far, [got[0], got[1]])


def solution(mesh):
    return jax.shard_map(
        functools.partial(shards, mesh.shape["row"], mesh.shape["col"]),
        mesh=mesh,
        in_specs=(P(None, AXES), P(None, AXES), P(), P("row", "col"), P(), P()),
        out_specs=P("row", "col"),
        check_vma=False,
    )
```

```python
import functools

import jax
import jax.numpy as jnp
from jax import lax
from jax.experimental import pallas as pl
from jax.experimental.pallas import tpu as pltpu
from jax.sharding import PartitionSpec as P

ORB = 128
NR = 16
AXES = ("row", "col")
VMEM_BYTES = 127 * 512 * 1024
EDGE_CHUNK = 256
BYTES_PER_US = 1_500_000
STEPS = ((0,), 1, 0, (1,))
CUTS = (6, 2)
PLAN = {
    'density_b_across_rows_2': ('raw_a_across_rows_1', 'raw_a_across_rows_2', 'raw_a_beside'),
    'far_2_3_across_cores': ('near_1_beside', 'near_1_direct'),
    'wide_b_across_cores': ('density_b_across_rows_1', 'density_b_across_rows_2'),
}


def taking(microseconds):
    return pl.CostEstimate(flops=0, bytes_accessed=int(microseconds * BYTES_PER_US), transcendentals=0)


def prepare_kernel(cells, chunks, atoms, atoms_total, edges, corner, coefficient, hits, embedding):
    count = edges.shape[1]
    size = count // chunks
    vec = edges[0:3, :]
    squared = vec[0:1] * vec[0:1] + vec[1:2] * vec[1:2] + vec[2:3] * vec[2:3]
    radius = jnp.sqrt(squared + 0.25)
    x, y, z = vec[0:1] / radius, vec[1:2] / radius, vec[2:3] / radius
    harmonics = jnp.concatenate(
        [jnp.ones_like(x), x, y, z, x * y, y * z, z * x, x * x - y * y, 3.0 * z * z - 1.0], axis=0
    )
    for k in range(NR):
        away = (radius - (1.0 + 0.3 * k)) / 0.5
        embedding[9 * k : 9 * k + 9, :] = jnp.exp(-(away * away)) * harmonics

    flipped = edges[...].T
    first, second = flipped[:, 3:4], flipped[:, 4:5]
    position = first * atoms_total + second
    position_row = edges[3:4, :] * atoms_total + edges[4:5, :]
    same = position == position_row
    coefficient[...] = lax.dot_general(
        same.astype(jnp.float32),
        embedding[...],
        (((1,), (1,)), ((), ())),
        precision=lax.Precision.HIGHEST,
        preferred_element_type=jnp.float32,
    ).astype(jnp.bfloat16)
    before = lax.broadcasted_iota(jnp.int32, (count, count), 1) < lax.broadcasted_iota(jnp.int32, (count, count), 0)
    repeated = jnp.max(jnp.where(same & before, 1.0, 0.0), axis=1, keepdims=True)

    mirrored = corner[2:3, :]
    row = first + mirrored * (second - first) - corner[0:1, :]
    col = second + mirrored * (first - second) - corner[1:2, :]
    limit = float(atoms)
    found = (row >= 0) & (row < limit) & (col >= 0) & (col < limit) & (corner[3:4, :] > 0) & (repeated < 0.5)
    found = jnp.where(found, 1.0, 0.0)
    lanes = lax.broadcasted_iota(jnp.int32, (1, ORB), 1).astype(jnp.float32)
    index = lax.broadcasted_iota(jnp.int32, (size, 1), 0).astype(jnp.float32)
    upto = lax.broadcasted_iota(jnp.int32, (size, size), 1) <= lax.broadcasted_iota(jnp.int32, (size, size), 0)
    upto = jnp.where(upto, 1.0, 0.0).astype(jnp.bfloat16)
    for chunk in range(chunks):
        part = slice(chunk * size, (chunk + 1) * size)
        here = found[part]
        place = jnp.dot(upto, here.astype(jnp.bfloat16), preferred_element_type=jnp.float32)
        code = (index * 2 + mirrored) * 4096 + row[part] * 64 + col[part]
        place = jnp.where(here > 0.5, place - 1.0, -1000.0)
        total = jnp.sum(here, axis=0, keepdims=True)
        for cell in range(cells):
            other = cells + cell
            direct = total[:, cell : cell + 1]
            at = jnp.where(place[:, cell : cell + 1] == lanes, code[:, cell : cell + 1], 0.0)
            at = at + jnp.where(place[:, other : other + 1] + direct == lanes, code[:, other : other + 1], 0.0)
            codes = jnp.sum(at, axis=0, keepdims=True)
            codes = jnp.where(lanes == ORB - 1, direct + total[:, other : other + 1], codes)
            hits[chunk, cell : cell + 1, :] = codes.astype(jnp.int32)


def cell_table(corner):
    cells = corner.shape[1]
    once = jnp.concatenate([corner, jnp.zeros((1, cells), jnp.int32), jnp.ones((1, cells), jnp.int32)])
    twice = jnp.concatenate([corner, jnp.ones((2, cells), jnp.int32)])
    table = jnp.concatenate([once, twice], axis=1).astype(jnp.float32)
    return jnp.pad(table, ((0, 4), (0, ORB - 2 * cells)))


def prepare(edges, table, cells, atoms, atoms_total):
    count = edges.shape[1]
    chunks = max(1, count // EDGE_CHUNK)
    return pl.pallas_call(
        functools.partial(prepare_kernel, cells, chunks, atoms, atoms_total),
        out_shape=[
            jax.ShapeDtypeStruct((count, 9 * NR), jnp.bfloat16),
            jax.ShapeDtypeStruct((chunks, cells, ORB), jnp.int32),
        ],
        scratch_shapes=[pltpu.VMEM((9 * NR, count), jnp.float32)],
        cost_estimate=taking(3),
        compiler_params=pltpu.CompilerParams(vmem_limit_bytes=VMEM_BYTES),
    )(edges, table)


def density_kernel(chunks, sources, unread, base, hits, scale, corner, coefficient, weight, *refs):
    cells = len(sources)
    refs = list(refs)
    raw = [[refs.pop(0) for _ in range(n)] for n in sources]
    refs = refs[unread:]
    out, (raw_in, total, ready, blocks, sems) = refs[:cells], refs[cells:]
    size = coefficient.shape[0] // chunks
    side = total.shape[0]
    wide = 8
    pitch = ORB + 8
    copies = []
    for n, refs_of in enumerate(raw):
        ways = [pltpu.make_async_copy(ref, raw_in.at[n], sems.at[0, n]) for ref in refs_of]
        copies.append(ways[0])
        if len(ways) == 1:
            ways[0].start()
        else:
            pl.when(scale[2] > 0.5)(ways[0].start)
            pl.when(scale[2] < 0.5)(ways[1].start)
    inverse = scale[1]

    def expand(chunk):
        def step(i, _):
            at = pl.multiple_of(i * (ORB * wide), ORB * wide)
            value = jnp.dot(
                coefficient[pl.ds(chunk * size, size), :],
                weight[:, pl.ds(at, ORB * wide)],
                preferred_element_type=jnp.float32,
            )
            for part in range(wide):
                blocks[pl.ds(i * wide + part, size, stride=pitch), :] = value[:, part * ORB : (part + 1) * ORB]
            return 0

        lax.fori_loop(0, ORB // wide, step, 0)

    if chunks == 1:
        expand(0)
    writes = []
    for n in range(cells):
        copies[n].wait()

        def spread(i, _):
            at = pl.ds(pl.multiple_of(i * ORB, ORB), ORB)
            total[at, :] = raw_in[n, at, :].astype(jnp.float32) * (-inverse)
            return 0

        lax.fori_loop(0, side // ORB, spread, 0)

        @pl.when(corner[0, base + n] == corner[1, base + n])
        def _():
            rows = lax.broadcasted_iota(jnp.int32, (ORB, ORB), 0)
            cols = lax.broadcasted_iota(jnp.int32, (ORB, ORB), 1)
            unit = jnp.where(rows == cols, scale[0], jnp.float32(0.0))
            for at in range(0, side, ORB):
                total[at : at + ORB, at : at + ORB] += unit

        for chunk in range(chunks):
            if chunks > 1:
                expand(chunk)

            def scatter(t, _):
                hit = hits[chunk, base + n, t]
                col = pl.multiple_of((hit % 64) * ORB, ORB)
                row = pl.multiple_of((hit // 64 % 64) * ORB, ORB)
                pair = hit // 4096
                spot = (pl.ds(row, ORB), pl.ds(col, ORB))
                block = blocks[pl.ds(pl.multiple_of(pair // 2 * pitch, 8), ORB), :] * inverse

                @pl.when(pair % 2 == 0)
                def _():
                    total[spot] = total[spot] - block

                @pl.when(pair % 2 == 1)
                def _():
                    total[spot] = total[spot] - block.T

                return 0

            lax.fori_loop(0, hits[chunk, base + n, ORB - 1], scatter, 0)

        def finish(i, _):
            at = pl.ds(pl.multiple_of(i * ORB, ORB), ORB)
            ready[n, at, :] = total[at, :].astype(jnp.bfloat16)
            return 0

        lax.fori_loop(0, side // ORB, finish, 0)
        writes.append(pltpu.make_async_copy(ready.at[n], out[n], sems.at[1, n]))
        writes[-1].start()
    for write in writes:
        write.wait()


def densities(raw, base, corner, hits, scale, coefficient, weight, sooner):
    cells = len(raw)
    sources = [len(refs) for refs in raw]
    raw = [ref for refs in raw for ref in refs]
    side = raw[0].shape[0]
    edges = coefficient.shape[0]
    chunks = max(1, edges // EDGE_CHUNK)
    any_spec = pl.BlockSpec(memory_space=pl.ANY)
    return pl.pallas_call(
        functools.partial(density_kernel, chunks, sources, len(sooner), base),
        out_shape=[jax.ShapeDtypeStruct((side, side), jnp.bfloat16)] * cells,
        in_specs=[pl.BlockSpec(memory_space=pltpu.SMEM)] * 3
        + [pl.BlockSpec(memory_space=pltpu.VMEM)] * 2
        + [any_spec] * (len(raw) + len(sooner)),
        out_specs=[any_spec] * cells,
        scratch_shapes=[
            pltpu.VMEM((cells, side, side), jnp.bfloat16),
            pltpu.VMEM((side, side), jnp.float32),
            pltpu.VMEM((cells, side, side), jnp.bfloat16),
            pltpu.VMEM((edges // chunks * (ORB + 8), ORB), jnp.float32),
            pltpu.SemaphoreType.DMA((2, cells)),
        ],
        cost_estimate=taking(6 + 2.5 * cells),
        compiler_params=pltpu.CompilerParams(vmem_limit_bytes=VMEM_BYTES),
    )(hits, scale, corner, coefficient, weight, *raw, *sooner)


def add_product(total, left, right, transposed, fresh):
    rows = total.shape[0]
    block = rows // 2
    contract = (((1,), (1,)), ((), ())) if transposed else (((1,), (0,)), ((), ()))
    for start in range(0, rows, block):
        at = pl.ds(start, block)
        value = lax.dot_general(left[at, :], right[...], contract, preferred_element_type=jnp.float32)
        total[at, :] = value if fresh else total[at, :] + value


def near_kernel(sides, sources, seeded, last, unread, source, *refs):
    count = len(sides)
    refs = list(refs)
    tall = [refs.pop(0) for _ in range(count)]
    wide = [[refs.pop(0) for _ in range(sources)] for _ in range(2)]
    seed = refs.pop(0) if seeded else None
    refs = refs[unread:]
    total = refs.pop(0)
    *rounded, tall_in, wide_in, sems = refs
    waits = []
    for n in range(count):
        for s in range(sources):

            @pl.when(source[n] == s)
            def _():
                pltpu.make_async_copy(wide[sides[n]][s], wide_in.at[n], sems.at[n, 0]).start()

        here = [
            pltpu.make_async_copy(wide[sides[n]][0], wide_in.at[n], sems.at[n, 0]),
            pltpu.make_async_copy(tall[n], tall_in.at[n], sems.at[n, 1]),
        ]
        here[1].start()
        if seeded and n == 0:
            here.append(pltpu.make_async_copy(seed, total, sems.at[count, 0]))
            here[-1].start()
        waits.append(here)
    for n in range(count):
        for copy in waits[n]:
            copy.wait()
        add_product(total, wide_in.at[n], tall_in.at[n], False, n == 0 and not seeded)
    at = 0
    for piece in rounded:
        rows = piece.shape[0]
        piece[...] = total[at : at + rows, :].astype(jnp.bfloat16)
        at += rows


def near_share(source, tall, sides, wide, seed, last, sooner):
    cell = tall[0].shape
    sources = len(wide[0])
    count = len(tall)
    any_spec = pl.BlockSpec(memory_space=pl.ANY)
    operands = [source, *tall, *wide[0], *wide[1]]
    if seed is not None:
        operands.append(seed)
    operands += sooner
    shapes = [jax.ShapeDtypeStruct(cell, jnp.float32)]
    if last:
        shapes += [jax.ShapeDtypeStruct((rows, cell[1]), jnp.bfloat16) for rows in last]
    return pl.pallas_call(
        functools.partial(near_kernel, sides, sources, seed is not None, last, len(sooner)),
        out_shape=shapes,
        in_specs=[pl.BlockSpec(memory_space=pltpu.SMEM)] + [any_spec] * (len(operands) - 1),
        out_specs=[pl.BlockSpec(memory_space=pltpu.VMEM)] * len(shapes),
        scratch_shapes=[
            pltpu.VMEM((count,) + cell, jnp.bfloat16),
            pltpu.VMEM((count,) + cell, jnp.bfloat16),
            pltpu.SemaphoreType.DMA((count + 1, 2)),
        ],
        cost_estimate=taking(2 + 2.5 * count),
        compiler_params=pltpu.CompilerParams(vmem_limit_bytes=VMEM_BYTES),
    )(*operands)


def far_kernel(count, unread, *refs):
    cells = refs[: 2 + 2 * count]
    out, cells_in, total, sems = refs[2 + 2 * count + unread :]
    copies = [pltpu.make_async_copy(ref, cells_in.at[n], sems.at[n]) for n, ref in enumerate(cells)]
    for copy in copies:
        copy.start()
    copies[0].wait()
    copies[1].wait()
    for m in range(count):
        for q in range(2):
            n = 2 + 2 * m + q
            copies[n].wait()
            add_product(total, cells_in.at[q], cells_in.at[n], True, q == 0)
        out[m] = total[...].astype(jnp.bfloat16)


def far_share(own, tall, sooner):
    cell = own[0].shape
    count = len(tall) // 2
    items = 2 + 2 * count
    any_spec = pl.BlockSpec(memory_space=pl.ANY)
    return pl.pallas_call(
        functools.partial(far_kernel, count, len(sooner)),
        out_shape=jax.ShapeDtypeStruct((count,) + cell, jnp.bfloat16),
        in_specs=[any_spec] * (items + len(sooner)),
        out_specs=pl.BlockSpec(memory_space=pltpu.VMEM),
        scratch_shapes=[
            pltpu.VMEM((items,) + cell, jnp.bfloat16),
            pltpu.VMEM(cell, jnp.float32),
            pltpu.SemaphoreType.DMA((items,)),
        ],
        cost_estimate=taking(3 + 3 * count),
        compiler_params=pltpu.CompilerParams(vmem_limit_bytes=VMEM_BYTES),
    )(*own, *tall, *sooner)


def final_kernel(parts, pieces, slot, *refs):
    refs = list(refs)
    near = [refs.pop(0) for _ in range(2)]
    far = [[refs.pop(0) for _ in range(n)] for n in parts]
    opposite = [[refs.pop(0) for _ in range(n)] for n in pieces]
    out, near_in, far_in, opposite_in, sems = refs
    turn = pl.program_id(0)
    block = 128
    groups = len(far)
    copies = []
    for q in range(2):
        here = [pltpu.make_async_copy(near[q], near_in.at[q], sems.at[q, 0])]
        for n, share in enumerate(far):
            part = share[q].at[0] if len(share) == 2 else share[0].at[q]
            here.append(pltpu.make_async_copy(part, far_in.at[q, n], sems.at[q, 1 + n]))
        at = 0
        for n, piece in enumerate(opposite[q]):
            to = opposite_in.at[q, pl.ds(at, piece.shape[0])]
            here.append(pltpu.make_async_copy(piece, to, sems.at[q, 1 + groups + n]))
            at += piece.shape[0]
        copies.append(here)

    @pl.when(turn == 0)
    def _():
        for here in copies:
            for copy in here:
                copy.start()

    for q in range(2):

        @pl.when(turn == q)
        def _():
            for copy in copies[q]:
                copy.wait()

            def step(n, _):
                at = pl.ds(pl.multiple_of(n * block, block), block)
                value = near_in[q, at, :]
                for n in range(groups):
                    value = value + far_in[q, n, at, :].astype(jnp.float32)
                out[at, :] = value + opposite_in[q, :, at].astype(jnp.float32).T
                return 0

            lax.fori_loop(0, out.shape[0] // block, step, 0)


def final_sum(slot, near, far, opposite):
    side = near[0].shape[0]
    groups = len(far)
    operands = [*near, *[part for share in far for part in share], *opposite[0], *opposite[1]]
    return pl.pallas_call(
        functools.partial(final_kernel, [len(share) for share in far], [len(pieces) for pieces in opposite]),
        out_shape=jax.ShapeDtypeStruct((side, 2 * side), jnp.float32),
        grid_spec=pltpu.PrefetchScalarGridSpec(
            num_scalar_prefetch=1,
            grid=(2,),
            in_specs=[pl.BlockSpec(memory_space=pl.ANY)] * len(operands),
            out_specs=pl.BlockSpec((side, side), lambda t, s: (0, s[t])),
            scratch_shapes=[
                pltpu.VMEM((2, side, side), jnp.float32),
                pltpu.VMEM((2, groups, side, side), jnp.bfloat16),
                pltpu.VMEM((2, side, side), jnp.bfloat16),
                pltpu.SemaphoreType.DMA((2, groups + 3)),
            ],
        ),
        cost_estimate=taking(9),
        compiler_params=pltpu.CompilerParams(vmem_limit_bytes=VMEM_BYTES),
    )(slot, *operands)


def after(value, *earlier):
    return lax.optimization_barrier((value, *earlier))[0] if earlier else value


def shards(row_size, col_size, edge_vec, edge_atoms, block_weight, base, lower_bound, upper_bound):
    devices = row_size * col_size
    half_rows = row_size // 2
    half_cols = col_size // 2
    side = base.shape[0]
    atoms = side // ORB
    row = lax.axis_index("row")
    col = lax.axis_index("col")
    row_half, row_in = row // half_rows, row % half_rows
    col_half, col_in = col // half_cols, col % half_cols
    on_diagonal = row_half == col_half
    slots = jnp.stack([row_in % 2, 1 - row_in % 2]).astype(jnp.int32)

    def moves(where):
        pairs = []
        for r in range(row_size):
            for c in range(col_size):
                to = where(r // half_rows, r % half_rows, c // half_cols, c % half_cols)
                if to is not None:
                    h, i, y, k = to
                    pairs.append((r * col_size + c, (h * half_rows + i) * col_size + y * half_cols + k))
        return pairs

    made = {}

    def waits(what):
        return [made[name] for name in PLAN.get(what, ()) if name in made]

    def send(value, where, what):
        with jax.named_scope(what):
            made[what] = lax.ppermute(after(value, *waits(what)), AXES, moves(where))
        return made[what]

    def swap_rows(value, bit, what):
        return send(value, lambda h, i, y, k: (h, i ^ bit, y, k), f"{what}_across_rows_{bit}")

    def to_beside(value, from_diagonal, what):
        return send(value, lambda h, i, y, k: (h, i, 1 - y, k) if (h == y) == from_diagonal else None, what)

    raw = [lax.dynamic_slice(base, (0, slots[q] * side), (side, side)) for q in range(2)]
    singles = [1 << b for b in range(half_rows.bit_length() - 1)]
    others = [m for m in range(1, half_rows) if m & (m - 1)]

    span = upper_bound[0] - lower_bound[0]
    scale = jnp.stack([upper_bound[0] / span, 1.0 / span, on_diagonal.astype(jnp.float32)])

    def tall_corner(mask, q):
        return row_half * half_rows + (row_in ^ mask), 2 * col + slots[q]

    corners = [tall_corner(0, q) for q in range(2)] + [tall_corner(m, 0) for m in singles]
    corners += [(row, row_half * half_rows + 2 * col_in + slots[0])]
    corner = jnp.stack([jnp.stack([c[n] for c in corners]) for n in range(2)]).astype(jnp.int32) * atoms
    table = cell_table(corner)

    edges = jnp.concatenate(
        [edge_vec, edge_atoms.astype(jnp.float32), jnp.zeros((3, edge_vec.shape[1]), jnp.float32)], axis=0
    )
    raw_a = {0: raw[0]}

    def double(value, bit):
        arrived = lax.ppermute(value, AXES, [(d, d ^ bit) for d in range(devices)])
        return jnp.concatenate([value, arrived], axis=1)

    bit = devices // 2
    while bit > col_size:
        edges = double(edges, bit)
        bit //= 2
        edges = after(edges, *((raw[0], raw[1]) if bit == col_size else (table, scale, corner)))
    for mask in singles[1:]:
        raw_a[mask] = swap_rows(after(raw[0], edges), mask, "raw_a")
    edges = double(edges, col_size)
    raw_a[1] = swap_rows(after(raw[1], edges), 1, "raw_a")
    bit = col_size // 2
    while bit >= half_cols:
        edges = double(edges, bit)
        bit //= 2
    beside_a = to_beside(after(raw[0], edges), True, "raw_a_beside")
    while bit:
        edges = double(edges, bit)
        bit //= 2

    done = []
    sums = []
    beside = []

    coefficient, hits = prepare(edges, table, len(corners), atoms, atoms * row_size)

    def density(cells, at):
        what = f"density_{at}"
        with jax.named_scope(what):
            got = densities(cells, at, corner, hits, scale, coefficient, block_weight, [*done[-1:], *waits(what)])
        done.append(got[0])
        return got

    tall = {mask: [None, None] for mask in range(half_rows)}
    def near_part(q):
        straight = CUTS[q] * side // 6
        pieces = [rows for rows in (straight, side - straight) if rows]
        what = f"near_{q}"
        place = after((row_in // 2) ^ col_in, *waits(what + "_source"))
        source = jnp.stack([place ^ (m // 2) for m in range(half_rows)]).astype(jnp.int32)
        sides = tuple(m % 2 for m in range(half_rows))
        with jax.named_scope(what):
            got = near_share(source, [tall[m][q] for m in tall], sides, wide, None, pieces, [*done[-1:], *waits(what)])
        done.append(got[0])
        made[what] = got[1]
        return got[0], got[1:]

    def far_product(masks):
        what = "far_" + "_".join(map(str, masks))
        with jax.named_scope(what):
            part = far_share(own, [tall[m][q] for m in masks for q in range(2)], [*done[-1:], *waits(what)])
        done.append(part)
        made[what] = part
        return part

    def far_sum(masks, part):
        what = "far_" + "_".join(map(str, masks))
        owner = lambda i: (i // 2) ^ (masks[0] // 2)
        summed = part.astype(jnp.float32)
        for turn in range(1, half_cols):
            arrived = send(
                part,
                lambda h, i, y, k: (h, i, y, owner(i)) if h != y and k == owner(i) ^ turn else None,
                what + "_across_cores",
            )
            summed = summed + arrived.astype(jnp.float32)
        across = lambda h, i, y, k: (h, i, 1 - y, k) if h != y and k == owner(i) else None
        summed = summed.astype(jnp.bfloat16)
        if masks[0] == 0:
            return [send(summed, across, f"{what}_beside")]
        return [send(summed[n : n + 1], across, f"{what}_beside_{n}") for n in range(2)]

    tall[0] = density([[cell] for cell in raw], 0)
    own = tall[0]
    tall[1][1] = swap_rows(own[0], 1, "density_b")
    beside_b = to_beside(own[1], True, "density_b_beside")
    for mask in singles[1:]:
        tall[mask][1] = swap_rows(own[1], mask, "density_b")
    got = density([[raw_a[m]] for m in singles] + [[raw[0], beside_a]], 2)
    for mask, value in zip(singles, got):
        tall[mask][0] = value
    wide = [[got[len(singles)]], [jnp.where(on_diagonal, own[1], beside_b)]]
    for group, name in zip(wide, ("a", "b")):
        for turn in range(1, half_cols):
            across = lambda h, i, y, k: (h, i, y, k ^ turn)
            group.append(send(group[0], across, f"wide_{name}_across_cores"))
    for mask in others:
        bit = 1 if mask ^ 1 in singles else mask & ~1 & -(mask & ~1)
        tall[mask][1] = swap_rows(tall[mask ^ bit][0 if bit == 1 else 1], bit, "forward_b")
        bit = 1 << (mask.bit_length() - 1)
        tall[mask][0] = swap_rows(tall[mask ^ bit][0], bit, "forward_a")

    def opposite(h, i, y, k, turn):
        return (1 - h, k * 2 + (i + turn) % 2, h, i // 2)

    def exchange(pieces_out, turn, cut):
        across = lambda h, i, y, k: opposite(h, i, y, k, turn) if h != y else None
        onward = lambda h, i, y, k: opposite(h, i, 1 - y, k, turn) if h == y else None
        pieces = []
        if cut > 0:
            pieces.append(send(pieces_out[0], across, f"near_{turn}_direct"))
        if cut < side:
            ahead = to_beside(pieces_out[-1], False, f"near_{turn}_beside")
            pieces.append(send(ahead, onward, f"near_{turn}_ahead"))
        return pieces

    near, got, parts, far = {}, {}, [], []
    for step in STEPS:
        if isinstance(step, int):
            near[step], value = near_part(step)
            got[step] = exchange(value, step, CUTS[step] * side // 6)
        else:
            for m in range(0, half_rows, 2):
                if min(m // 2, 1) in step:
                    parts.append(([m, m + 1], far_product([m, m + 1])))
    for masks, part in parts:
        far.append(far_sum(masks, part))
    return final_sum(slots, [near[0], near[1]], far, [got[0], got[1]])


def solution(mesh):
    return jax.shard_map(
        functools.partial(shards, mesh.shape["row"], mesh.shape["col"]),
        mesh=mesh,
        in_specs=(P(None, AXES), P(None, AXES), P(), P("row", "col"), P(), P()),
        out_specs=P("row", "col"),
        check_vma=False,
    )
```
